256 devices in a mesh: tm: 32 (over x, z), height: 4 (over y_hi, core), heads: 2 (over y_lo).
Axes of the slice: x: 4, y: 4 (y_hi: 2, y_lo: 2; y = y_hi * 2 + y_lo), z: 8, core: 2. Of those that a mesh axis runs over, the one named last changes fastest.
Arguments:
- queries: bfloat16 [192, 32, 8, 768], P('tm', 'height', None, 'heads'), may hold values from -18 to 18
- key_tokens: bfloat16 [192, 32, 8, 768], P('tm', 'height', None, 'heads'), may hold values from -4 to 4
- value_tokens: bfloat16 [192, 32, 8, 768], P('tm', 'height', None, 'heads'), may hold values from -5 to 5
- cotangent: bfloat16 [192, 32, 8, 768], P('tm', 'height', None, 'heads'), may hold values from -5 to 5
- window_mask: int32 [32, 4, 9], replicated, may hold values 0 or 1
Outputs:
- attended: bfloat16 [192, 32, 8, 768], P('tm', 'height', None, 'heads')
- query_grad: bfloat16 [192, 32, 8, 768], P('tm', 'height', None, 'heads')
- key_grad: bfloat16 [192, 32, 8, 768], P('tm', 'height', None, 'heads')
- value_grad: bfloat16 [192, 32, 8, 768], P('tm', 'height', None, 'heads')
The draws below stay inside these ranges and needn't reach their ends.
All inputs are finite; a program needn't handle non-finite values.
Results may differ from the reference program's by a relative error of at most 0.012.
Values may be sent and summed in bfloat16 or wider, within the bound.
A program may use at most 128 MiB of HBM per device.

```python
import jax
import jax.numpy as jnp
from jax import lax

HEADS = 12
HEAD_DIM = 64
TILE_T = 6
TILE_H = 8
TILE_W = 8
TILE = 384
FEAT = 768
TTILES = 32
HTILES = 4
FRAMES = 192
ROWS = 32


def draw_queries(key, part):
    key = jax.random.fold_in(key, 1)
    drawn = jax.random.truncated_normal(key, -4.0, 4.0, (FRAMES, ROWS, TILE_W, FEAT), jnp.float32)
    return drawn.astype(jnp.bfloat16)


def draw_key_tokens(key, part):
    key = jax.random.fold_in(key, 2)
    drawn = jax.random.truncated_normal(key, -4.0, 4.0, (FRAMES, ROWS, TILE_W, FEAT), jnp.float32)
    return drawn.astype(jnp.bfloat16)


def place_ends(result, rng, smallest, high):
    spot = [jax.random.randint(jax.random.fold_in(rng, axis), (), 0, length) for axis, length in enumerate(result.shape)]
    widest = result.shape.index(max(result.shape))
    beside = spot[:widest] + [(spot[widest] + 1) % result.shape[widest]] + spot[widest + 1:]
    return result.at[tuple(spot)].set(smallest).at[tuple(beside)].set(high)


def levels(rng, dims, shards, smallest, top_value):
    def one(dim, shards_of):
        heights = jax.random.uniform(jax.random.fold_in(jax.random.fold_in(rng, 6), dim), (shards_of,), jnp.float32, smallest / len(shards), top_value / len(shards))
        return jnp.repeat(jnp.exp(heights), dims[dim] // shards_of).reshape((-1,) + (1,) * (len(dims) - dim - 1))

    gain = one(*shards[0])
    for cut in shards[1:]:
        gain = gain * one(*cut)
    return gain


def bell_draw(stream_key, shape, deviation, most, cuts=(), held_as=jnp.bfloat16):
    gain = levels(stream_key, shape, cuts, -0.22, 0.18) if cuts else 1.0
    drawn = jax.random.normal(stream_key, shape, jnp.float32) * deviation * gain
    return jnp.minimum(jnp.maximum(drawn, -most), most).astype(held_as)


def setup_inputs(seed: int = 0) -> dict:
    splits = jax.random.split(jax.random.key(seed), 6)
    return {
        "queries": draw_queries(jax.random.fold_in(splits[5], 71), 0),
        "key_tokens": draw_key_tokens(jax.random.fold_in(splits[5], 71), 0),
        "value_tokens": bell_draw(splits[2], (FRAMES, ROWS, TILE_W, FEAT), 1.0, 5.0, ((0, 32), (1, 4), (3, 2))),
        "cotangent": bell_draw(splits[3], (FRAMES, ROWS, TILE_W, FEAT), 1.0, 5.0, ((0, 32), (1, 4), (3, 2))),
        "window_mask": place_ends((jax.random.randint(splits[4], (TTILES, HTILES, 9), 0, 3) < 2).astype(jnp.int32), jax.random.fold_in(splits[4], 1), 0, 1),
    }


masked_score = -1e30


def to_tiles(grid):
    shaped = grid.reshape(TTILES, TILE_T, HTILES, TILE_H, TILE_W, FEAT)
    return shaped.transpose(0, 2, 1, 3, 4, 5).reshape(TTILES, HTILES, TILE, FEAT)


def to_grid(tiles):
    shaped = tiles.reshape(TTILES, HTILES, TILE_T, TILE_H, TILE_W, FEAT)
    return shaped.transpose(0, 2, 1, 3, 4, 5).reshape(FRAMES, ROWS, TILE_W, FEAT)


def border(tiles):
    widths = [(1, 1), (1, 1)] + [(0, 0)] * (tiles.ndim - 2)
    return jnp.pad(tiles, widths)


def block_of(padded, row_tile, column_tile):
    starts = (row_tile, column_tile) + (jnp.int32(0),) * (padded.ndim - 2)
    return lax.dynamic_slice(padded, starts, (3, 3) + padded.shape[2:])


def rounded(values):
    return lax.optimization_barrier(values.astype(jnp.bfloat16)).astype(jnp.float32)


def validity(window_mask):
    tile_time = jnp.arange(TTILES, dtype=jnp.int32)[:, None, None]
    tile_height = jnp.arange(HTILES, dtype=jnp.int32)[None, :, None]
    offset = jnp.arange(9, dtype=jnp.int32)[None, None, :]
    time_index = tile_time + offset // 3 - 1
    height_index = tile_height + offset % 3 - 1
    inside = (time_index >= 0) & (time_index < TTILES) & (height_index >= 0) & (height_index < HTILES)
    return inside & ((offset == 4) | (window_mask == 1))


def reference(queries, key_tokens, value_tokens, cotangent, window_mask):
    scale = HEAD_DIM ** -0.5
    query_tiles = to_tiles(queries)
    key_tiles = to_tiles(key_tokens)
    value_tiles = to_tiles(value_tokens)
    grad_tiles = to_tiles(cotangent)
    allowed = validity(window_mask)
    key_pad = border(key_tiles)
    value_pad = border(value_tiles)
    indices = jnp.arange(TTILES * HTILES, dtype=jnp.int32)

    def query_side(index):
        row_tile = index // HTILES
        column_tile = index % HTILES
        query = query_tiles[row_tile, column_tile].reshape(TILE, HEADS, HEAD_DIM).astype(jnp.float32)
        grads = grad_tiles[row_tile, column_tile].reshape(TILE, HEADS, HEAD_DIM).astype(jnp.float32)
        keys_near = block_of(key_pad, row_tile, column_tile).reshape(9 * TILE, HEADS, HEAD_DIM).astype(jnp.float32)
        values_near = block_of(value_pad, row_tile, column_tile).reshape(9 * TILE, HEADS, HEAD_DIM).astype(jnp.float32)
        usable = jnp.repeat(allowed[row_tile, column_tile], TILE)
        scores = jnp.einsum("qhd,khd->hqk", query, keys_near) * scale
        scores = jnp.where(usable[None, None, :], scores, masked_score)
        highest = jnp.max(scores, axis=-1, keepdims=True)
        logsum = highest + jnp.log(jnp.sum(jnp.exp(scores - highest), axis=-1, keepdims=True))
        weights = jnp.exp(scores - logsum)
        output = jnp.einsum("hqk,khd->qhd", rounded(weights), values_near).astype(jnp.bfloat16)
        carried = jnp.sum(grads * output.astype(jnp.float32), axis=-1).T
        product = jnp.einsum("qhd,khd->hqk", grads, values_near)
        slopes = rounded(weights * (product - carried[:, :, None]) * scale)
        query_grad = jnp.einsum("hqk,khd->qhd", slopes, keys_near).astype(jnp.bfloat16)
        return output.reshape(TILE, FEAT), query_grad.reshape(TILE, FEAT), logsum[:, :, 0], carried

    attended, query_grad, logsum, carried = lax.map(query_side, indices)
    logsum = logsum.reshape(TTILES, HTILES, HEADS, TILE)
    carried = carried.reshape(TTILES, HTILES, HEADS, TILE)
    query_pad = border(query_tiles)
    grad_pad = border(grad_tiles)
    logsum_pad = border(logsum)
    carried_pad = border(carried)
    allowed_pad = border(allowed)

    def key_side(index):
        row_tile = index // HTILES
        column_tile = index % HTILES
        own_keys = key_tiles[row_tile, column_tile].reshape(TILE, HEADS, HEAD_DIM).astype(jnp.float32)
        own_values = value_tiles[row_tile, column_tile].reshape(TILE, HEADS, HEAD_DIM).astype(jnp.float32)
        sources = block_of(query_pad, row_tile, column_tile)[::-1, ::-1].reshape(9 * TILE, HEADS, HEAD_DIM).astype(jnp.float32)
        grads = block_of(grad_pad, row_tile, column_tile)[::-1, ::-1].reshape(9 * TILE, HEADS, HEAD_DIM).astype(jnp.float32)
        logsums = block_of(logsum_pad, row_tile, column_tile)[::-1, ::-1].transpose(2, 0, 1, 3).reshape(HEADS, 9 * TILE)
        carries = block_of(carried_pad, row_tile, column_tile)[::-1, ::-1].transpose(2, 0, 1, 3).reshape(HEADS, 9 * TILE)
        flags = block_of(allowed_pad, row_tile, column_tile)[::-1, ::-1].reshape(9, 9)
        usable = jnp.repeat(jnp.diagonal(flags), TILE)
        scores = jnp.einsum("qhd,khd->hqk", sources, own_keys) * scale
        scores = jnp.where(usable[None, :, None], scores, masked_score)
        weights = jnp.exp(scores - logsums[:, :, None])
        value_grad = jnp.einsum("hqk,qhd->khd", rounded(weights), grads).astype(jnp.bfloat16)
        product = jnp.einsum("qhd,khd->hqk", grads, own_values)
        slopes = rounded(weights * (product - carries[:, :, None]) * scale)
        key_grad = jnp.einsum("hqk,qhd->khd", slopes, sources).astype(jnp.bfloat16)
        return key_grad.reshape(TILE, FEAT), value_grad.reshape(TILE, FEAT)

    key_grad, value_grad = lax.map(key_side, indices)
    shape = (TTILES, HTILES, TILE, FEAT)
    return (to_grid(attended.reshape(shape)), to_grid(query_grad.reshape(shape)), to_grid(key_grad.reshape(shape)), to_grid(value_grad.reshape(shape)))
```

```python
import functools

import jax
import jax.numpy as jnp
from jax import lax
from jax.experimental import pallas as pl
from jax.experimental.pallas import tpu as pltpu
from jax.sharding import PartitionSpec as P

MESH = pl.DeviceIdType.MESH
F32 = jnp.float32
BF16 = jnp.bfloat16
DIM = 64
TILE = 384
HEADS = 6
NEAR = 3
FAR = 1e30


def swap_halves(x):
    return pltpu.roll(x, DIM, 1)


def kernel(
    tiles_t,
    mask_ref, q_ref, k_ref, v_ref, g_ref,
    att_ref, qg_ref, kg_ref, vg_ref,
    kv_own, qd_own, kv, qd, dkv, terms, oq, oq_all,
    e_s, eh_s, ds_s, w_s, ot_s, m_s, l_s, qt_s, dqt_s, kvt_s,
    kv_send, kv_recv, qd_send, qd_recv, dkv_send, dkv_recv, oq_send, oq_recv,
):
    t = lax.axis_index("tm")
    h = lax.axis_index("height")
    hi = h // 2
    core = h % 2
    inner = jnp.where(hi == 0, core, 1 - core)
    sibling = 2 * hi + 1 - core
    outer_h, inner_h, partner_h = 3 * hi, 1 + hi, 2 - hi
    heights = (outer_h, inner_h, partner_h)
    has = {-1: t > 0, 0: t >= 0, 1: t < tiles_t - 1}

    barrier = pltpu.get_barrier_semaphore()
    for dt in (-1, 0, 1):
        @pl.when(has[dt])
        def _():
            for dh in range(1 if dt == 0 else 0, 4):
                pl.semaphore_signal(
                    barrier, inc=1, device_id={"tm": t + dt, "height": lax.rem(h + dh, 4)}, device_id_type=MESH
                )

    lane = lax.broadcasted_iota(jnp.int32, (TILE, 2 * DIM), 1)
    low = lane < DIM

    def pack(pair, _):
        cols = pl.ds(pl.multiple_of(pair * 2 * DIM, 2 * DIM), 2 * DIM)
        for own, a_ref, b_ref, factor in ((kv_own, k_ref, v_ref, 1.0), (qd_own, q_ref, g_ref, 0.125)):
            a = a_ref[:, cols].astype(F32) * factor
            b = b_ref[:, cols].astype(F32)
            own[2 * pair] = jnp.where(low, a, swap_halves(b)).astype(BF16)
            own[2 * pair + 1] = jnp.where(low, swap_halves(a), b).astype(BF16)
        return 0

    lax.fori_loop(0, HEADS // 2, pack, 0)
    for dt in (-1, 1):
        @pl.when(jnp.logical_not(has[dt]))
        def _():
            for n in range(NEAR):
                for u in range(3):
                    kv[n, 3 * (dt + 1) + u] = jnp.zeros((TILE, 2 * DIM), BF16)
            for n in range(HEADS):
                terms[n, 1 + dt] = jnp.zeros((TILE, 2 * DIM), BF16)
                terms[n, 4 + dt] = jnp.zeros((TILE, 2 * DIM), BF16)
    for n in range(NEAR):
        kv[n, 3 + inner] = kv_own[3 * core + n]
        qd[n, inner] = qd_own[3 * core + n]
    count = 4 * (1 + (t > 0).astype(jnp.int32) + (t < tiles_t - 1).astype(jnp.int32)) - 1
    pl.semaphore_wait(barrier, count)

    def qd_copy(n):
        return pltpu.make_async_remote_copy(
            src_ref=qd_own.at[3 * (1 - core) + n], dst_ref=qd.at[n, inner],
            send_sem=qd_send.at[n], recv_sem=qd_recv.at[n],
            device_id={"height": sibling}, device_id_type=MESH,
        )

    def kv_copy(n, dt, far, to):
        chip = 1 - hi if far else hi
        slot = 3 * (1 - dt) + (2 if far else inner)
        return pltpu.make_async_remote_copy(
            src_ref=kv_own.at[3 * to + n], dst_ref=kv.at[n, slot],
            send_sem=kv_send.at[n, (dt + 1) * 4 + 2 * far + (0 if isinstance(to, int) and to == 0 else 1)],
            recv_sem=kv_recv.at[n, slot],
            device_id={"tm": t + dt, "height": 2 * chip + to}, device_id_type=MESH,
        )

    def each_kv(n, act, with_centre=True):
        act(kv_copy(n, 0, 0, 1 - core))
        for dt in (-1, 1):
            @pl.when(has[dt])
            def _():
                for to in range(2):
                    act(kv_copy(n, dt, 0, to))
        for dt in (0, -1, 1):
            @pl.when((inner == 1) & has[dt])
            def _():
                for to in range(2):
                    act(kv_copy(n, dt, 1, to))

    def send_head(n, _):
        qd_copy(n).start()
        each_kv(n, lambda c: c.start())
        return 0

    lax.fori_loop(0, NEAR, send_head, 0)

    def wait_kv(n, slot):
        pltpu.make_async_remote_copy(
            src_ref=kv_own.at[0], dst_ref=kv.at[n, slot], send_sem=kv_send.at[0, 0], recv_sem=kv_recv.at[n, slot],
            device_id={"height": sibling}, device_id_type=MESH,
        ).wait_recv()

    def allowed(dt, u):
        def one(query_h, key_h):
            o = 3 * (dt + 1) + key_h - query_h + 1
            flag = mask_ref[(t * 4 + query_h) * 9 + o]
            flag = jnp.where(o == 4, 1, flag)
            return jnp.where(has[dt], flag, 0)

        inner_flag = one(inner_h, heights[u])
        if u == 2:
            return jnp.full((1, TILE), inner_flag, jnp.int32)
        spot = lax.broadcasted_iota(jnp.int32, (1, 2 * TILE), 1)
        return jnp.where(spot < TILE, one(outer_h, heights[u]), inner_flag)

    def slots(group):
        return [3 * group, 3 * group + 1] if group < 3 else [2, 5, 8]

    def keys(n, group):
        if group < 3:
            return kv[n, 3 * group:3 * group + 2].reshape(2 * TILE, 2 * DIM)
        return jnp.concatenate([kv[n, j] for j in slots(3)], 0)

    def forward(n, group):
        js = slots(group)
        first = 0 if group < 3 else TILE
        for j in js:
            kvt_s[n, j] = kv[n, j].astype(F32).T.astype(BF16)
        scores = jnp.dot(keys(n, group), qt_s[n, 0, :, first:], preferred_element_type=F32)
        flags = [allowed(j // 3 - 1, j % 3) > 0 for j in js]
        tops = [
            jnp.where(flag, jnp.max(scores[i * TILE:(i + 1) * TILE], axis=0, keepdims=True), -FAR)
            for i, flag in enumerate(flags)
        ]
        top = functools.reduce(jnp.maximum, tops)
        total = 0.0
        parts = []
        for i, flag in enumerate(flags):
            e = jnp.exp(scores[i * TILE:(i + 1) * TILE] - jnp.where(flag, top, FAR))
            total = total + jnp.sum(e, axis=0, keepdims=True)
            parts.append(e.astype(BF16))
        e = jnp.concatenate(parts, 0)
        if group < 3:
            e_s[n, group] = e
        else:
            eh_s[...] = e
        values = jnp.concatenate([kvt_s[n, j, DIM:] for j in js], 1)
        ot_s[n, group, :, first:] = jnp.dot(values, e, preferred_element_type=F32)
        m_s[n, group:group + 1, first:] = top
        l_s[n, group:group + 1, first:] = total

    def centre(n, _):
        wait_kv(n, 4 - inner)
        qd_copy(n).wait_recv()
        turned = qd[n].reshape(2 * TILE, 2 * DIM).astype(F32).T
        zero = jnp.zeros((DIM, 2 * TILE), BF16)
        qt_s[n, 0] = jnp.concatenate([turned[:DIM].astype(BF16), zero], 0)
        qt_s[n, 1] = jnp.concatenate([zero, turned[DIM:].astype(BF16)], 0)
        forward(n, 1)
        return 0

    lax.fori_loop(0, NEAR, centre, 0)

    def dkv_copy(n, dt, u):
        return pltpu.make_async_remote_copy(
            src_ref=dkv.at[n, 3 * (dt + 1) + u], dst_ref=terms.at[3 * core + n, (4 if u == 2 else 1) - dt],
            send_sem=dkv_send.at[n, 3 * (dt + 1) + u], recv_sem=dkv_recv.at[3 * core + n, (4 if u == 2 else 1) - dt],
            device_id={"tm": t + dt, "height": heights[u]}, device_id_type=MESH,
        )

    def dkv_near_copy(n):
        return pltpu.make_async_remote_copy(
            src_ref=dkv.at[n, 4 - inner], dst_ref=terms.at[3 * core + n, 1],
            send_sem=dkv_send.at[n, 4], recv_sem=dkv_recv.at[3 * core + n, 1],
            device_id={"height": sibling}, device_id_type=MESH,
        )

    def oq_copy(n):
        return pltpu.make_async_remote_copy(
            src_ref=oq.at[n, 1 - inner], dst_ref=oq_all.at[3 * core + n],
            send_sem=oq_send.at[n], recv_sem=oq_recv.at[n],
            device_id={"height": sibling}, device_id_type=MESH,
        )

    def head(n, _):
        for dt in (-1, 1):
            @pl.when(has[dt])
            def _():
                wait_kv(n, 3 * (dt + 1))
                wait_kv(n, 3 * (dt + 1) + 1)
            forward(n, dt + 1)
        for dt in (-1, 0, 1):
            @pl.when(has[dt])
            def _():
                wait_kv(n, 3 * (dt + 1) + 2)
        forward(n, 3)
        m_s[n, 3:4, :TILE] = jnp.full((1, TILE), -FAR, F32)
        l_s[n, 3:4, :TILE] = jnp.zeros((1, TILE), F32)
        tops = m_s[n, 0:4]
        shares = jnp.exp(tops - jnp.max(tops, axis=0, keepdims=True))
        shares = shares / jnp.sum(shares * l_s[n, 0:4], axis=0, keepdims=True)
        out = ot_s[n, 0] * shares[0:1] + ot_s[n, 1] * shares[1:2] + ot_s[n, 2] * shares[2:3]
        out = jnp.concatenate([out[:, :TILE], out[:, TILE:] + ot_s[n, 3, :, TILE:] * shares[3:4, TILE:]], 1)
        out = out.astype(BF16).astype(F32)
        carried = jnp.sum(qt_s[n, 1, DIM:].astype(F32) * out, axis=0, keepdims=True)

        def backward(group):
            first = 0 if group < 3 else TILE
            size = 768 if group < 3 else 1152
            js = slots(group)
            product = jnp.dot(keys(n, group), qt_s[n, 1, :, first:], preferred_element_type=F32)
            e = e_s[n, group] if group < 3 else eh_s[...]
            weights = e.astype(F32) * shares[group:group + 1, first:]
            slopes = (weights * (product - carried[:, first:])).astype(BF16)
            ds_s[:size, first:] = slopes
            w_s[:size, first:] = weights.astype(BF16)
            turned = jnp.concatenate([kvt_s[n, j, :DIM] for j in js], 1)
            part = jnp.dot(turned, slopes, preferred_element_type=F32)
            if group == 0:
                dqt_s[...] = part
            else:
                dqt_s[:, first:] += part
            rhs = qd[n].reshape(2 * TILE, 2 * DIM)[first:]
            key_part = jnp.dot(ds_s[:size, first:], rhs, preferred_element_type=F32)
            value_part = jnp.dot(w_s[:size, first:], rhs, preferred_element_type=F32)
            lanes = lax.broadcasted_iota(jnp.int32, (size, 2 * DIM), 1)
            both = jnp.where(lanes < DIM, key_part, value_part).astype(BF16)
            for i, j in enumerate(js):
                dkv[n, j] = both[i * TILE:(i + 1) * TILE]

        for dt in (-1, 1):
            backward(dt + 1)
            @pl.when(has[dt])
            def _():
                for u in range(2):
                    dkv_copy(n, dt, u).start()
        backward(3)
        for dt in (-1, 0, 1):
            @pl.when(has[dt])
            def _():
                dkv_copy(n, dt, 2).start()
        backward(1)
        dkv_near_copy(n).start()
        terms[3 * core + n, 1] = dkv[n, 3 + inner]
        both = jnp.concatenate([out, dqt_s[...] * 0.125], 0).T.astype(BF16)
        oq[n, 0] = both[:TILE]
        oq[n, 1] = both[TILE:]
        oq_copy(n).start()
        oq_all[3 * core + n] = oq[n, inner]
        return 0

    lax.fori_loop(0, NEAR, head, 0)

    def wait_term(n, term):
        pltpu.make_async_remote_copy(
            src_ref=dkv.at[0, 0], dst_ref=terms.at[n, term], send_sem=dkv_send.at[0, 0], recv_sem=dkv_recv.at[n, term],
            device_id={"height": sibling}, device_id_type=MESH,
        ).wait_recv()

    for n in range(NEAR):
        pltpu.make_async_remote_copy(
            src_ref=oq.at[n, 0], dst_ref=oq_all.at[3 * (1 - core) + n], send_sem=oq_send.at[n], recv_sem=oq_recv.at[n],
            device_id={"height": sibling}, device_id_type=MESH,
        ).wait_recv()
        wait_term(3 * (1 - core) + n, 1)
        for c in range(2):
            for dt in (-1, 1):
                @pl.when(has[dt])
                def _():
                    wait_term(3 * c + n, 1 + dt)
            for dt in (-1, 0, 1):
                @pl.when(has[dt] & (inner == 1))
                def _():
                    wait_term(3 * c + n, 4 + dt)

    def finish(pair, _):
        cols = pl.ds(pl.multiple_of(pair * 2 * DIM, 2 * DIM), 2 * DIM)

        def store(even, odd, a_ref, b_ref):
            a_ref[:, cols] = jnp.where(low, even, swap_halves(odd)).astype(BF16)
            b_ref[:, cols] = jnp.where(low, swap_halves(even), odd).astype(BF16)

        store(oq_all[2 * pair].astype(F32), oq_all[2 * pair + 1].astype(F32), att_ref, qg_ref)

        def summed(n, count):
            total = terms[n, 0].astype(F32)
            for i in range(1, count):
                total = total + terms[n, i].astype(F32)
            return total

        @pl.when(inner == 1)
        def _():
            store(summed(2 * pair, 6), summed(2 * pair + 1, 6), kg_ref, vg_ref)

        @pl.when(inner == 0)
        def _():
            store(summed(2 * pair, 3), summed(2 * pair + 1, 3), kg_ref, vg_ref)

        return 0

    lax.fori_loop(0, HEADS // 2, finish, 0)

    def drain(n, _):
        qd_copy(n).wait_send()
        each_kv(n, lambda c: c.wait_send())
        for dt in (-1, 1):
            @pl.when(has[dt])
            def _():
                for u in range(2):
                    dkv_copy(n, dt, u).wait_send()
        for dt in (-1, 0, 1):
            @pl.when(has[dt])
            def _():
                dkv_copy(n, dt, 2).wait_send()
        dkv_near_copy(n).wait_send()
        oq_copy(n).wait_send()
        return 0

    lax.fori_loop(0, NEAR, drain, 0)


def local(tiles_t, queries, key_tokens, value_tokens, cotangent, window_mask):
    flat = (TILE, HEADS * DIM)
    vmem = pl.BlockSpec(memory_space=pltpu.VMEM)
    block = (TILE, 2 * DIM)
    dma = pltpu.SemaphoreType.DMA
    outs = pl.pallas_call(
        functools.partial(kernel, tiles_t),
        out_shape=[jax.ShapeDtypeStruct(flat, BF16)] * 4,
        in_specs=[pl.BlockSpec(memory_space=pltpu.SMEM)] + [vmem] * 4,
        out_specs=[vmem] * 4,
        scratch_shapes=[
            pltpu.VMEM((HEADS, *block), BF16),
            pltpu.VMEM((HEADS, *block), BF16),
            pltpu.VMEM((NEAR, 9, *block), BF16),
            pltpu.VMEM((NEAR, 2, *block), BF16),
            pltpu.VMEM((NEAR, 9, *block), BF16),
            pltpu.VMEM((HEADS, 6, *block), BF16),
            pltpu.VMEM((NEAR, 2, *block), BF16),
            pltpu.VMEM((HEADS, *block), BF16),
            pltpu.VMEM((NEAR, 3, 768, 768), BF16),
            pltpu.VMEM((1152, 384), BF16),
            pltpu.VMEM((1152, 768), BF16),
            pltpu.VMEM((1152, 768), BF16),
            pltpu.VMEM((NEAR, 4, DIM, 768), F32),
            pltpu.VMEM((NEAR, 8, 768), F32),
            pltpu.VMEM((NEAR, 8, 768), F32),
            pltpu.VMEM((NEAR, 2, 2 * DIM, 768), BF16),
            pltpu.VMEM((DIM, 768), F32),
            pltpu.VMEM((NEAR, 9, 2 * DIM, TILE), BF16),
            dma((NEAR, 12)),
            dma((NEAR, 9)),
            dma((NEAR,)),
            dma((NEAR,)),
            dma((NEAR, 9)),
            dma((HEADS, 6)),
            dma((NEAR,)),
            dma((NEAR,)),
        ],
        compiler_params=pltpu.CompilerParams(
            collective_id=0, has_side_effects=True, vmem_limit_bytes=60 * 1024 * 1024
        ),
    )(
        window_mask.reshape(-1),
        queries.reshape(flat), key_tokens.reshape(flat), value_tokens.reshape(flat), cotangent.reshape(flat),
    )
    return tuple(out.reshape(queries.shape) for out in outs)


def solution(mesh):
    spec = P("tm", "height", None, "heads")
    return jax.shard_map(
        functools.partial(local, mesh.shape["tm"]), mesh=mesh, in_specs=(spec,) * 4 + (P(),), out_specs=(spec,) * 4,
        check_vma=False,
    )
```

```python
import functools

import jax
import jax.numpy as jnp
from jax import lax
from jax.experimental import pallas as pl
from jax.experimental.pallas import tpu as pltpu
from jax.sharding import PartitionSpec as P

MESH = pl.DeviceIdType.MESH
F32 = jnp.float32
BF16 = jnp.bfloat16
DIM = 64
TILE = 384
HEADS = 6
NEAR = 3
FAR = 1e30


def swap_halves(x):
    return pltpu.roll(x, DIM, 1)


def kernel(
    tiles_t,
    mask_hbm, q_hbm, k_hbm, v_hbm, g_hbm,
    att_ref, qg_ref, kg_ref, vg_ref,
    arrays, mask_s, flag_s, kv_own, qd_own, kv, qd, dkv, y_back, z_back, terms, oq, oq_all,
    e_s, eh_s, ds_s, w_s, ot_s, m_s, l_s, qt_s, dqt_s, kvt_s,
    load_sem, kv_send, kv_recv, pass_send, qd_send, qd_recv, dkv_send, dkv_recv, y_recv, z_recv, oq_send, oq_recv,
):
    t = lax.axis_index("tm")
    h = lax.axis_index("height")
    hi = h // 2
    core = h % 2
    inner = jnp.where(hi == 0, core, 1 - core)
    sibling = 2 * hi + 1 - core
    outer_h, inner_h, partner_h = 3 * hi, 1 + hi, 2 - hi
    heights = (outer_h, inner_h, partner_h)
    has = {-1: t > 0, 0: t >= 0, 1: t < tiles_t - 1}

    barrier = pltpu.get_barrier_semaphore()
    for dt in (-1, 0, 1):
        @pl.when(has[dt])
        def _():
            for height in (h, sibling) if dt else (sibling, 2 - 2 * hi, 3 - 2 * hi):
                pl.semaphore_signal(barrier, inc=1, device_id={"tm": t + dt, "height": height}, device_id_type=MESH)

    loads = [
        pltpu.make_async_copy(ref, arrays.at[i], load_sem.at[i]) for i, ref in enumerate((k_hbm, v_hbm, q_hbm, g_hbm))
    ] + [pltpu.make_async_copy(mask_hbm, mask_s, load_sem.at[4])]
    for load in loads:
        load.start()

    lane = lax.broadcasted_iota(jnp.int32, (TILE, 2 * DIM), 1)
    low = lane < DIM
    for load in loads[:2]:
        load.wait()

    def pack(own, first, factor, pair, _):
        cols = pl.ds(pl.multiple_of(pair * 2 * DIM, 2 * DIM), 2 * DIM)
        a = arrays[first, :, cols].astype(F32) * factor
        b = arrays[first + 1, :, cols].astype(F32)
        own[2 * pair] = jnp.where(low, a, swap_halves(b)).astype(BF16)
        own[2 * pair + 1] = jnp.where(low, swap_halves(a), b).astype(BF16)
        return 0

    lax.fori_loop(0, HEADS // 2, functools.partial(pack, kv_own, 0, 1.0), 0)
    for load in loads[2:]:
        load.wait()
    lax.fori_loop(0, HEADS // 2, functools.partial(pack, qd_own, 2, 0.125), 0)
    for dt in (-1, 1):
        @pl.when(jnp.logical_not(has[dt]))
        def _():
            for n in range(NEAR):
                for u in range(3):
                    kv[n, 3 * (dt + 1) + u] = jnp.zeros((TILE, 2 * DIM), BF16)
            for n in range(HEADS):
                terms[n, 1 + dt] = jnp.zeros((TILE, 2 * DIM), BF16)
            for n in range(2):
                z_back[n, (1 + dt) // 2] = jnp.zeros((TILE, 2 * DIM), BF16)
    for n in range(NEAR):
        kv[n, 3 + inner] = kv_own[3 * core + n]
        qd[n, inner] = qd_own[3 * core + n]
    spot = lax.broadcasted_iota(jnp.int32, (9, 4, tiles_t), 2)
    row = lax.broadcasted_iota(jnp.int32, (9, 4, tiles_t), 1)
    for i, query_h in enumerate((outer_h, inner_h)):
        chosen = jnp.where((spot == t) & (row == query_h), mask_s[...], 0).astype(F32)
        chosen = jnp.sum(jnp.sum(chosen, axis=2, keepdims=True), axis=1, keepdims=True)
        flag_s[i] = jnp.broadcast_to(chosen, (9, 1, 2 * DIM))

    count = 3 + 2 * ((t > 0).astype(jnp.int32) + (t < tiles_t - 1).astype(jnp.int32))
    pl.semaphore_wait(barrier, count)

    def qd_copy(n):
        return pltpu.make_async_remote_copy(
            src_ref=qd_own.at[3 * (1 - core) + n], dst_ref=qd.at[n, inner],
            send_sem=qd_send.at[n], recv_sem=qd_recv.at[n],
            device_id={"height": sibling}, device_id_type=MESH,
        )

    def kv_copy(n, dt, to, far=0):
        slot = 3 * (1 - dt) + (2 if far else inner)
        index = 5 + to if far else {-1: to, 0: 2, 1: 3 + to}[dt]
        return pltpu.make_async_remote_copy(
            src_ref=kv_own.at[3 * to + n], dst_ref=kv.at[n, slot],
            send_sem=kv_send.at[n, index], recv_sem=kv_recv.at[n, slot],
            device_id={"tm": t + dt, "height": 2 * (1 - hi if far else hi) + to}, device_id_type=MESH,
        )

    def kv_along(n, act):
        for dt in (-1, 1):
            @pl.when(has[dt])
            def _():
                for to in range(2):
                    act(kv_copy(n, dt, to))

    def kv_beside(n, act):
        act(kv_copy(n, 0, 1 - core))

        @pl.when(inner == 1)
        def _():
            for to in range(2):
                act(kv_copy(n, 0, to, 1))

    def pass_over(n, dt):
        slot = 3 * (dt + 1)
        return pltpu.make_async_remote_copy(
            src_ref=kv.at[n, slot + 1], dst_ref=kv.at[n, slot + 2],
            send_sem=pass_send.at[n, (dt + 1) // 2], recv_sem=kv_recv.at[n, slot + 2],
            device_id={"height": 2 * (1 - hi) + core}, device_id_type=MESH,
        )

    def pass_along(n, dt):
        slot = 3 * (1 - dt) + 2
        return pltpu.make_async_remote_copy(
            src_ref=kv.at[n, 5], dst_ref=kv.at[n, slot],
            send_sem=pass_send.at[n, (dt + 1) // 2], recv_sem=kv_recv.at[n, slot],
            device_id={"tm": t + dt}, device_id_type=MESH,
        )

    def send_head(n, _):
        qd_copy(n).start()
        kv_beside(n, lambda c: c.start())

        @pl.when(n < 2)
        def _():
            kv_along(n, lambda c: c.start())
        return 0

    lax.fori_loop(0, NEAR, send_head, 0)

    def wait_kv(n, slot):
        pltpu.make_async_remote_copy(
            src_ref=kv_own.at[0], dst_ref=kv.at[n, slot], send_sem=kv_send.at[0, 0], recv_sem=kv_recv.at[n, slot],
            device_id={"height": sibling}, device_id_type=MESH,
        ).wait_recv()

    def passes_along(n):
        wait_kv(n, 5)
        for dt in (-1, 1):
            @pl.when(has[dt])
            def _():
                pass_along(n, dt).start()

    def allowed(dt, u):
        def one(i, query_h, key_h):
            if dt == 0 and i == u:
                return jnp.ones((1, TILE), F32)
            flag = flag_s[i, 3 * (dt + 1) + key_h - query_h + 1] * has[dt].astype(F32)
            return jnp.concatenate([flag] * 3, 1)

        inner_flag = one(1, inner_h, heights[u])
        if u == 2:
            return inner_flag
        return jnp.concatenate([one(0, outer_h, heights[u]), inner_flag], 1)

    def slots(group):
        return [3 * group, 3 * group + 1] if group < 3 else [2, 5, 8]

    def keys(n, group):
        if group < 3:
            return kv[n, 3 * group:3 * group + 2].reshape(2 * TILE, 2 * DIM)
        return jnp.concatenate([kv[n, j] for j in slots(3)], 0)

    def forward(n, group):
        js = slots(group)
        first = 0 if group < 3 else TILE
        for j in js:
            kvt_s[n, j] = kv[n, j].astype(F32).T.astype(BF16)
        scores = jnp.dot(keys(n, group), qt_s[n, 0, :, first:], preferred_element_type=F32)
        flags = [allowed(j // 3 - 1, j % 3) > 0 for j in js]
        tops = [
            jnp.where(flag, jnp.max(scores[i * TILE:(i + 1) * TILE], axis=0, keepdims=True), -FAR)
            for i, flag in enumerate(flags)
        ]
        top = functools.reduce(jnp.maximum, tops)
        total = 0.0
        parts = []
        for i, flag in enumerate(flags):
            e = jnp.exp(scores[i * TILE:(i + 1) * TILE] - jnp.where(flag, top, FAR))
            total = total + jnp.sum(e, axis=0, keepdims=True)
            parts.append(e.astype(BF16))
        e = jnp.concatenate(parts, 0)
        if group < 3:
            e_s[n, group] = e
        else:
            eh_s[...] = e
        values = jnp.concatenate([kvt_s[n, j, DIM:] for j in js], 1)
        ot_s[n, group, :, first:] = jnp.dot(values, e, preferred_element_type=F32)
        m_s[n, group:group + 1, first:] = top
        l_s[n, group:group + 1, first:] = total

    def centre(n, _):
        wait_kv(n, 4 - inner)
        qd_copy(n).wait_recv()
        turned = qd[n].reshape(2 * TILE, 2 * DIM).astype(F32).T
        zero = jnp.zeros((DIM, 2 * TILE), BF16)
        qt_s[n, 0] = jnp.concatenate([turned[:DIM].astype(BF16), zero], 0)
        qt_s[n, 1] = jnp.concatenate([zero, turned[DIM:].astype(BF16)], 0)
        forward(n, 1)
        return 0

    lax.fori_loop(0, NEAR, centre, 0)
    passes_along(0)
    kv_along(2, lambda c: c.start())

    def dkv_copy(n, dt, u):
        term = 3 if u == 2 else 1 - dt
        return pltpu.make_async_remote_copy(
            src_ref=dkv.at[n, 3 * (dt + 1) + u], dst_ref=terms.at[3 * core + n, term],
            send_sem=dkv_send.at[n, 3 * (dt + 1) + u], recv_sem=dkv_recv.at[3 * core + n, term],
            device_id={"tm": t + dt, "height": heights[u]}, device_id_type=MESH,
        )

    def over_copy(n, dt):
        return pltpu.make_async_remote_copy(
            src_ref=dkv.at[n, 3 * (dt + 1) + 2], dst_ref=y_back.at[(dt + 1) // 2],
            send_sem=dkv_send.at[n, 3 * (dt + 1) + 2], recv_sem=y_recv.at[(dt + 1) // 2],
            device_id={"height": 2 * (1 - hi) + core}, device_id_type=MESH,
        )

    def along_copy(n, dt):
        return pltpu.make_async_remote_copy(
            src_ref=dkv.at[n, 3 * (dt + 1) + 2], dst_ref=z_back.at[n, (1 - dt) // 2],
            send_sem=dkv_send.at[n, 3 * (dt + 1) + 2], recv_sem=z_recv.at[n, (1 - dt) // 2],
            device_id={"tm": t + dt}, device_id_type=MESH,
        )

    def add_along(n):
        for i, dt in enumerate((-1, 1)):
            @pl.when(has[dt])
            def _():
                pltpu.make_async_remote_copy(
                    src_ref=dkv.at[0, 0], dst_ref=z_back.at[n, i], send_sem=dkv_send.at[0, 0],
                    recv_sem=z_recv.at[n, i], device_id={"height": sibling}, device_id_type=MESH,
                ).wait_recv()
        dkv[n, 5] = (dkv[n, 5].astype(F32) + z_back[n, 0].astype(F32) + z_back[n, 1].astype(F32)).astype(BF16)
        dkv_copy(n, 0, 2).start()

    def add_over(n):
        for i, dt in enumerate((-1, 1)):
            @pl.when(has[dt])
            def _():
                pltpu.make_async_remote_copy(
                    src_ref=dkv.at[0, 0], dst_ref=y_back.at[i], send_sem=dkv_send.at[0, 0],
                    recv_sem=y_recv.at[i], device_id={"height": sibling}, device_id_type=MESH,
                ).wait_recv()
                slot = 3 * (dt + 1) + 1
                dkv[n, slot] = (dkv[n, slot].astype(F32) + y_back[i].astype(F32)).astype(BF16)
                dkv_copy(n, dt, 1).start()

    def dkv_near_copy(n):
        return pltpu.make_async_remote_copy(
            src_ref=dkv.at[n, 4 - inner], dst_ref=terms.at[3 * core + n, 1],
            send_sem=dkv_send.at[n, 4], recv_sem=dkv_recv.at[3 * core + n, 1],
            device_id={"height": sibling}, device_id_type=MESH,
        )

    def oq_copy(n):
        return pltpu.make_async_remote_copy(
            src_ref=oq.at[n, 1 - inner], dst_ref=oq_all.at[3 * core + n],
            send_sem=oq_send.at[n], recv_sem=oq_recv.at[n],
            device_id={"height": sibling}, device_id_type=MESH,
        )

    def backward(n, group):
        first = 0 if group < 3 else TILE
        size = 768 if group < 3 else 1152
        js = slots(group)
        product = jnp.dot(keys(n, group), qt_s[n, 1, :, first:], preferred_element_type=F32)
        e = e_s[n, group] if group < 3 else eh_s[...]
        weights = e.astype(F32) * m_s[n, group:group + 1, first:]
        slopes = (weights * (product - m_s[n, 4:5, first:])).astype(BF16)
        ds_s[:size, first:] = slopes
        w_s[:size, first:] = weights.astype(BF16)
        turned = jnp.concatenate([kvt_s[n, j, :DIM] for j in js], 1)
        part = jnp.dot(turned, slopes, preferred_element_type=F32)
        if group == 3:
            dqt_s[n, :, :TILE] = jnp.zeros((DIM, TILE), F32)
            dqt_s[n, :, TILE:] = part
        else:
            dqt_s[n, :, first:] += part
        rhs = qd[n].reshape(2 * TILE, 2 * DIM)[first:]
        key_part = jnp.dot(ds_s[:size, first:], rhs, preferred_element_type=F32)
        value_part = jnp.dot(w_s[:size, first:], rhs, preferred_element_type=F32)
        lanes = lax.broadcasted_iota(jnp.int32, (size, 2 * DIM), 1)
        both = jnp.where(lanes < DIM, key_part, value_part)
        both = both.astype(BF16)
        for i, j in enumerate(js):
            dkv[n, j] = both[i * TILE:(i + 1) * TILE]

    def groups(n):
        for dt in (-1, 1):
            @pl.when(has[dt])
            def _():
                wait_kv(n, 3 * (dt + 1))
                wait_kv(n, 3 * (dt + 1) + 1)

            @pl.when(has[dt] & (n == 1))
            def _():
                pass_over(1, dt).start()
            forward(n, dt + 1)
            if dt < 0:
                @pl.when(n == 1)
                def _():
                    passes_along(2)

    def head(n):
        @pl.when(n == 1)
        def _():
            wait_kv(n, 5)
        for dt in (-1, 1):
            @pl.when(has[dt])
            def _():
                wait_kv(n, 3 * (dt + 1) + 2)
        forward(n, 3)
        m_s[n, 3:4, :TILE] = jnp.full((1, TILE), -FAR, F32)
        l_s[n, 3:4, :TILE] = jnp.zeros((1, TILE), F32)
        tops = m_s[n, 0:4]
        shares = jnp.exp(tops - jnp.max(tops, axis=0, keepdims=True))
        shares = shares / jnp.sum(shares * l_s[n, 0:4], axis=0, keepdims=True)
        out = ot_s[n, 0] * shares[0:1] + ot_s[n, 1] * shares[1:2] + ot_s[n, 2] * shares[2:3]
        out = jnp.concatenate([out[:, :TILE], out[:, TILE:] + ot_s[n, 3, :, TILE:] * shares[3:4, TILE:]], 1)
        out = out.astype(BF16).astype(F32)
        ot_s[n, 0] = out
        m_s[n, 0:4] = shares
        m_s[n, 4:5] = jnp.sum(qt_s[n, 1, DIM:].astype(F32) * out, axis=0, keepdims=True)

        @pl.when(n == 1)
        def _():
            add_along(0)

        backward(n, 3)
        for dt in (-1, 1):
            @pl.when(has[dt] & (n < 2))
            def _():
                along_copy(n, dt).start()

            @pl.when(has[dt] & (n == 2))
            def _():
                over_copy(n, dt).start()

    def sides(n, _):
        for dt in (-1, 1):
            backward(n, dt + 1)

            @pl.when(has[dt])
            def _():
                dkv_copy(n, dt, 0).start()

            @pl.when(has[dt] & (n < 2))
            def _():
                dkv_copy(n, dt, 1).start()
        return 0

    def step(i, _):
        @pl.when(i < NEAR)
        def _():
            groups(i)

        @pl.when(i > 0)
        def _():
            head(i - 1)
        lax.fori_loop(jnp.where(i == NEAR, 1, 0), jnp.where(i == NEAR, NEAR, i % 2), sides, 0)
        return 0

    lax.fori_loop(0, NEAR + 1, step, 0)

    def last(n, _):
        @pl.when(n == 0)
        def _():
            add_along(1)

        @pl.when(n == 1)
        def _():
            dkv_copy(2, 0, 2).start()
            add_over(2)
        backward(n, 1)
        dkv_near_copy(n).start()
        terms[3 * core + n, 1] = dkv[n, 3 + inner]
        both = jnp.concatenate([ot_s[n, 0], dqt_s[n] * 0.125], 0).T.astype(BF16)
        oq[n, 0] = both[:TILE]
        oq[n, 1] = both[TILE:]
        oq_copy(n).start()
        oq_all[3 * core + n] = oq[n, inner]
        return 0

    lax.fori_loop(0, NEAR, last, 0)

    def wait_terms(n):
        wait_term(3 * (1 - core) + n, 1)
        for c in range(2):
            for dt in (-1, 1):
                @pl.when(has[dt])
                def _():
                    wait_term(3 * c + n, 1 + dt)

            @pl.when(inner == 1)
            def _():
                wait_term(3 * c + n, 3)

    def wait_term(n, term):
        pltpu.make_async_remote_copy(
            src_ref=dkv.at[0, 0], dst_ref=terms.at[n, term], send_sem=dkv_send.at[0, 0], recv_sem=dkv_recv.at[n, term],
            device_id={"height": sibling}, device_id_type=MESH,
        ).wait_recv()

    def store(pair, even, odd, a, b):
        cols = slice(pair * 2 * DIM, (pair + 1) * 2 * DIM)
        a[:, cols] = jnp.where(low, even, swap_halves(odd)).astype(BF16)
        b[:, cols] = jnp.where(low, swap_halves(even), odd).astype(BF16)

    def summed(n, from_partner):
        total = terms[n, 0].astype(F32)
        for i in range(1, 4 if from_partner else 3):
            total = total + terms[n, i].astype(F32)
        return total

    def store_sums(pair):
        for side in range(2):
            @pl.when(inner == side)
            def _():
                store(pair, summed(2 * pair, side), summed(2 * pair + 1, side), kg_ref, vg_ref)

    for n in range(NEAR):
        pltpu.make_async_remote_copy(
            src_ref=oq.at[n, 0], dst_ref=oq_all.at[3 * (1 - core) + n], send_sem=oq_send.at[n], recv_sem=oq_recv.at[n],
            device_id={"height": sibling}, device_id_type=MESH,
        ).wait_recv()
    for pair in range(HEADS // 2):
        store(pair, oq_all[2 * pair].astype(F32), oq_all[2 * pair + 1].astype(F32), att_ref, qg_ref)
    wait_terms(0)
    wait_terms(1)
    store_sums(0)
    wait_terms(2)
    store_sums(1)
    store_sums(2)

    def drain(n, _):
        qd_copy(n).wait_send()
        kv_beside(n, lambda c: c.wait_send())
        kv_along(n, lambda c: c.wait_send())
        for dt in (-1, 1):
            @pl.when(has[dt])
            def _():
                for u in range(3):
                    dkv_copy(n, dt, u).wait_send()

                pass_over(n, dt).wait_send()
        dkv_copy(n, 0, 2).wait_send()
        dkv_near_copy(n).wait_send()
        oq_copy(n).wait_send()
        return 0

    lax.fori_loop(0, NEAR, drain, 0)


def handed_on(*refs):
    copies = [pltpu.make_async_copy(refs[i], refs[4 + i], refs[8].at[i]) for i in range(4)]
    for copy in copies:
        copy.start()
    for copy in copies:
        copy.wait()


def local(tiles_t, queries, key_tokens, value_tokens, cotangent, window_mask):
    flat = (TILE, HEADS * DIM)
    anywhere = pl.BlockSpec(memory_space=pl.ANY)
    block = (TILE, 2 * DIM)
    dma = pltpu.SemaphoreType.DMA
    outs = pl.pallas_call(
        functools.partial(kernel, tiles_t),
        out_shape=[pltpu.VMEM(flat, BF16)] * 4,
        in_specs=[anywhere] * 5,
        out_specs=[pl.BlockSpec(memory_space=pltpu.VMEM)] * 4,
        scratch_shapes=[
            pltpu.VMEM((4, *flat), BF16),
            pltpu.VMEM((9, 4, tiles_t), jnp.int32),
            pltpu.VMEM((2, 9, 1, 2 * DIM), F32),
            pltpu.VMEM((HEADS, *block), BF16),
            pltpu.VMEM((HEADS, *block), BF16),
            pltpu.VMEM((NEAR, 9, *block), BF16),
            pltpu.VMEM((NEAR, 2, *block), BF16),
            pltpu.VMEM((NEAR, 9, *block), BF16),
            pltpu.VMEM((2, *block), BF16),
            pltpu.VMEM((2, 2, *block), BF16),
            pltpu.VMEM((HEADS, 4, *block), BF16),
            pltpu.VMEM((NEAR, 2, *block), BF16),
            pltpu.VMEM((HEADS, *block), BF16),
            pltpu.VMEM((NEAR, 3, 768, 768), BF16),
            pltpu.VMEM((1152, 384), BF16),
            pltpu.VMEM((1152, 768), BF16),
            pltpu.VMEM((1152, 768), BF16),
            pltpu.VMEM((NEAR, 4, DIM, 768), F32),
            pltpu.VMEM((NEAR, 8, 768), F32),
            pltpu.VMEM((NEAR, 8, 768), F32),
            pltpu.VMEM((NEAR, 2, 2 * DIM, 768), BF16),
            pltpu.VMEM((NEAR, DIM, 768), F32),
            pltpu.VMEM((NEAR, 9, 2 * DIM, TILE), BF16),
            dma((5,)),
            dma((NEAR, 7)),
            dma((NEAR, 9)),
            dma((NEAR, 2)),
            dma((NEAR,)),
            dma((NEAR,)),
            dma((NEAR, 9)),
            dma((HEADS, 4)),
            dma((2,)),
            dma((2, 2)),
            dma((NEAR,)),
            dma((NEAR,)),
        ],
        compiler_params=pltpu.CompilerParams(
            collective_id=0, has_side_effects=True, vmem_limit_bytes=56 * 1024 * 1024
        ),
    )(
        window_mask.transpose(2, 1, 0),
        queries.reshape(flat), key_tokens.reshape(flat), value_tokens.reshape(flat), cotangent.reshape(flat),
    )
    outs = pl.pallas_call(
        handed_on,
        out_shape=[jax.ShapeDtypeStruct(flat, BF16)] * 4,
        in_specs=[pl.BlockSpec(memory_space=pltpu.VMEM)] * 4,
        out_specs=[anywhere] * 4,
        scratch_shapes=[dma((4,))],
    )(*(pltpu.with_memory_space_constraint(out, pltpu.VMEM) for out in outs))
    return tuple(out.reshape(queries.shape) for out in outs)


def solution(mesh):
    spec = P("tm", "height", None, "heads")
    return jax.shard_map(
        functools.partial(local, mesh.shape["tm"]), mesh=mesh, in_specs=(spec,) * 4 + (P(),), out_specs=(spec,) * 4,
        check_vma=False,
    )
```

```python
import functools

import jax
import jax.numpy as jnp
from jax import lax
from jax.experimental import pallas as pl
from jax.experimental.pallas import tpu as pltpu
from jax.sharding import PartitionSpec as P

MESH = pl.DeviceIdType.MESH
F32 = jnp.float32
BF16 = jnp.bfloat16
DIM = 64
TILE = 384
HEADS = 6
NEAR = 3
FAR = 1e30


def swap_halves(x):
    return pltpu.roll(x, DIM, 1)


def kernel(
    tiles_t,
    mask_hbm, q_hbm, k_hbm, v_hbm, g_hbm,
    att_ref, qg_ref, kg_ref, vg_ref,
    arrays, mask_s, flag_s, kv_own, qd_own, kv, qd, dkv, y_back, z_back, terms, oq, oq_all,
    e_s, eh_s, ds_s, w_s, ot_s, m_s, l_s, qt_s, dqt_s, kvt_s,
    load_sem, kv_send, kv_recv, pass_send, qd_send, qd_recv, dkv_send, dkv_recv, y_recv, z_recv, oq_send, oq_recv,
):
    t = lax.axis_index("tm")
    h = lax.axis_index("height")
    hi = h // 2
    core = h % 2
    inner = jnp.where(hi == 0, core, 1 - core)
    sibling = 2 * hi + 1 - core
    outer_h, inner_h, partner_h = 3 * hi, 1 + hi, 2 - hi
    heights = (outer_h, inner_h, partner_h)
    has = {-1: t > 0, 0: t >= 0, 1: t < tiles_t - 1}

    barrier = pltpu.get_barrier_semaphore()
    for dt in (-1, 0, 1):
        @pl.when(has[dt])
        def _():
            for height in (h, sibling) if dt else (sibling, 2 - 2 * hi, 3 - 2 * hi):
                pl.semaphore_signal(barrier, inc=1, device_id={"tm": t + dt, "height": height}, device_id_type=MESH)

    loads = [
        pltpu.make_async_copy(ref, arrays.at[i], load_sem.at[i]) for i, ref in enumerate((k_hbm, v_hbm, q_hbm, g_hbm))
    ] + [pltpu.make_async_copy(mask_hbm, mask_s, load_sem.at[4])]
    for load in loads:
        load.start()

    lane = lax.broadcasted_iota(jnp.int32, (TILE, 2 * DIM), 1)
    low = lane < DIM
    for load in loads[:2]:
        load.wait()

    def pack(own, first, factor, pair, _):
        cols = pl.ds(pl.multiple_of(pair * 2 * DIM, 2 * DIM), 2 * DIM)
        a = arrays[first, :, cols].astype(F32) * factor
        b = arrays[first + 1, :, cols].astype(F32)
        own[2 * pair] = jnp.where(low, a, swap_halves(b)).astype(BF16)
        own[2 * pair + 1] = jnp.where(low, swap_halves(a), b).astype(BF16)
        return 0

    lax.fori_loop(0, HEADS // 2, functools.partial(pack, kv_own, 0, 1.0), 0)
    for dt in (-1, 1):
        @pl.when(jnp.logical_not(has[dt]))
        def _():
            for n in range(NEAR):
                for u in range(3):
                    kv[n, 3 * (dt + 1) + u] = jnp.zeros((TILE, 2 * DIM), BF16)
            for n in range(HEADS):
                terms[n, 1 + dt] = jnp.zeros((TILE, 2 * DIM), BF16)
            for n in range(2):
                z_back[n, (1 + dt) // 2] = jnp.zeros((TILE, 2 * DIM), BF16)
    for n in range(NEAR):
        kv[n, 3 + inner] = kv_own[3 * core + n]
    count = 3 + 2 * ((t > 0).astype(jnp.int32) + (t < tiles_t - 1).astype(jnp.int32))
    pl.semaphore_wait(barrier, count)

    def qd_copy(n):
        return pltpu.make_async_remote_copy(
            src_ref=qd_own.at[3 * (1 - core) + n], dst_ref=qd.at[n, inner],
            send_sem=qd_send.at[n], recv_sem=qd_recv.at[n],
            device_id={"height": sibling}, device_id_type=MESH,
        )

    def kv_copy(n, dt, to, far=0):
        slot = 3 * (1 - dt) + (2 if far else inner)
        index = 5 + to if far else {-1: to, 0: 2, 1: 3 + to}[dt]
        return pltpu.make_async_remote_copy(
            src_ref=kv_own.at[3 * to + n], dst_ref=kv.at[n, slot],
            send_sem=kv_send.at[n, index], recv_sem=kv_recv.at[n, slot],
            device_id={"tm": t + dt, "height": 2 * (1 - hi if far else hi) + to}, device_id_type=MESH,
        )

    def kv_along(n, act):
        for dt in (-1, 1):
            @pl.when(has[dt])
            def _():
                for to in range(2):
                    act(kv_copy(n, dt, to))

    def kv_beside(n, act):
        act(kv_copy(n, 0, 1 - core))

        @pl.when(inner == 1)
        def _():
            for to in range(2):
                act(kv_copy(n, 0, to, 1))

    def pass_over(n, dt):
        slot = 3 * (dt + 1)
        return pltpu.make_async_remote_copy(
            src_ref=kv.at[n, slot + 1], dst_ref=kv.at[n, slot + 2],
            send_sem=pass_send.at[n, (dt + 1) // 2], recv_sem=kv_recv.at[n, slot + 2],
            device_id={"height": 2 * (1 - hi) + core}, device_id_type=MESH,
        )

    def pass_along(n, dt):
        slot = 3 * (1 - dt) + 2
        return pltpu.make_async_remote_copy(
            src_ref=kv.at[n, 5], dst_ref=kv.at[n, slot],
            send_sem=pass_send.at[n, (dt + 1) // 2], recv_sem=kv_recv.at[n, slot],
            device_id={"tm": t + dt}, device_id_type=MESH,
        )

    kv_along(0, lambda c: c.start())
    for n in range(NEAR):
        kv_beside(n, lambda c: c.start())
    kv_along(1, lambda c: c.start())
    for load in loads[2:]:
        load.wait()
    lax.fori_loop(0, HEADS // 2, functools.partial(pack, qd_own, 2, 0.125), 0)
    for n in range(NEAR):
        qd_copy(n).start()
        qd[n, inner] = qd_own[3 * core + n]
    spot = lax.broadcasted_iota(jnp.int32, (9, 4, tiles_t), 2)
    row = lax.broadcasted_iota(jnp.int32, (9, 4, tiles_t), 1)
    for i, query_h in enumerate((outer_h, inner_h)):
        chosen = jnp.where((spot == t) & (row == query_h), mask_s[...], 0).astype(F32)
        chosen = jnp.sum(jnp.sum(chosen, axis=2, keepdims=True), axis=1, keepdims=True)
        flag_s[i] = jnp.broadcast_to(chosen, (9, 1, 2 * DIM))


    def wait_kv(n, slot):
        pltpu.make_async_remote_copy(
            src_ref=kv_own.at[0], dst_ref=kv.at[n, slot], send_sem=kv_send.at[0, 0], recv_sem=kv_recv.at[n, slot],
            device_id={"height": sibling}, device_id_type=MESH,
        ).wait_recv()

    def passes_along(n):
        wait_kv(n, 5)
        for dt in (-1, 1):
            @pl.when(has[dt])
            def _():
                pass_along(n, dt).start()

    def allowed(dt, u):
        def one(i, query_h, key_h):
            if dt == 0 and i == u:
                return jnp.ones((1, TILE), F32)
            flag = flag_s[i, 3 * (dt + 1) + key_h - query_h + 1] * has[dt].astype(F32)
            return jnp.concatenate([flag] * 3, 1)

        inner_flag = one(1, inner_h, heights[u])
        if u == 2:
            return inner_flag
        return jnp.concatenate([one(0, outer_h, heights[u]), inner_flag], 1)

    def slots(group):
        return [3 * group, 3 * group + 1] if group < 3 else [2, 5, 8]

    def keys(n, group):
        if group < 3:
            return kv[n, 3 * group:3 * group + 2].reshape(2 * TILE, 2 * DIM)
        return jnp.concatenate([kv[n, j] for j in slots(3)], 0)

    def forward(n, group):
        js = slots(group)
        first = 0 if group < 3 else TILE
        for j in js:
            kvt_s[n, j] = kv[n, j].T
        scores = jnp.dot(keys(n, group), qt_s[n, 0, :, first:], preferred_element_type=F32)
        flags = [allowed(j // 3 - 1, j % 3) > 0 for j in js]
        tops = [
            jnp.where(flag, jnp.max(scores[i * TILE:(i + 1) * TILE], axis=0, keepdims=True), -FAR)
            for i, flag in enumerate(flags)
        ]
        top = functools.reduce(jnp.maximum, tops)
        total = 0.0
        parts = []
        for i, flag in enumerate(flags):
            e = jnp.exp(scores[i * TILE:(i + 1) * TILE] - jnp.where(flag, top, FAR))
            total = total + jnp.sum(e, axis=0, keepdims=True)
            parts.append(e.astype(BF16))
        e = jnp.concatenate(parts, 0)
        if group < 3:
            e_s[n, group] = e
        else:
            eh_s[...] = e
        values = jnp.concatenate([kvt_s[n, j, DIM:] for j in js], 1)
        ot_s[n, group, :, first:] = jnp.dot(values, e, preferred_element_type=F32)
        m_s[n, group:group + 1, first:] = top
        l_s[n, group:group + 1, first:] = total

    def centre(n, _):
        wait_kv(n, 4 - inner)
        qd_copy(n).wait_recv()
        turned = qd[n].reshape(2 * TILE, 2 * DIM).astype(F32).T
        zero = jnp.zeros((DIM, 2 * TILE), BF16)
        qt_s[n, 0] = jnp.concatenate([turned[:DIM].astype(BF16), zero], 0)
        qt_s[n, 1] = jnp.concatenate([zero, turned[DIM:].astype(BF16)], 0)
        forward(n, 1)
        return 0

    lax.fori_loop(0, NEAR, centre, 0)
    passes_along(0)

    def dkv_copy(n, dt, u):
        term = 3 if u == 2 else 1 - dt
        return pltpu.make_async_remote_copy(
            src_ref=dkv.at[n, 3 * (dt + 1) + u], dst_ref=terms.at[3 * core + n, term],
            send_sem=dkv_send.at[n, 3 * (dt + 1) + u], recv_sem=dkv_recv.at[3 * core + n, term],
            device_id={"tm": t + dt, "height": heights[u]}, device_id_type=MESH,
        )

    def over_copy(n, dt):
        return pltpu.make_async_remote_copy(
            src_ref=dkv.at[n, 3 * (dt + 1) + 2], dst_ref=y_back.at[(dt + 1) // 2],
            send_sem=dkv_send.at[n, 3 * (dt + 1) + 2], recv_sem=y_recv.at[(dt + 1) // 2],
            device_id={"height": 2 * (1 - hi) + core}, device_id_type=MESH,
        )

    def along_copy(n, dt):
        return pltpu.make_async_remote_copy(
            src_ref=dkv.at[n, 3 * (dt + 1) + 2], dst_ref=z_back.at[n, (1 - dt) // 2],
            send_sem=dkv_send.at[n, 3 * (dt + 1) + 2], recv_sem=z_recv.at[n, (1 - dt) // 2],
            device_id={"tm": t + dt}, device_id_type=MESH,
        )

    def add_along(n):
        for i, dt in enumerate((-1, 1)):
            @pl.when(has[dt])
            def _():
                pltpu.make_async_remote_copy(
                    src_ref=dkv.at[0, 0], dst_ref=z_back.at[n, i], send_sem=dkv_send.at[0, 0],
                    recv_sem=z_recv.at[n, i], device_id={"height": sibling}, device_id_type=MESH,
                ).wait_recv()
        dkv[n, 5] = (dkv[n, 5].astype(F32) + z_back[n, 0].astype(F32) + z_back[n, 1].astype(F32)).astype(BF16)
        dkv_copy(n, 0, 2).start()

    def add_over(n):
        for i, dt in enumerate((-1, 1)):
            @pl.when(has[dt])
            def _():
                pltpu.make_async_remote_copy(
                    src_ref=dkv.at[0, 0], dst_ref=y_back.at[i], send_sem=dkv_send.at[0, 0],
                    recv_sem=y_recv.at[i], device_id={"height": sibling}, device_id_type=MESH,
                ).wait_recv()
                slot = 3 * (dt + 1) + 1
                dkv[n, slot] = (dkv[n, slot].astype(F32) + y_back[i].astype(F32)).astype(BF16)
                dkv_copy(n, dt, 1).start()

    def dkv_near_copy(n):
        return pltpu.make_async_remote_copy(
            src_ref=dkv.at[n, 4 - inner], dst_ref=terms.at[3 * core + n, 1],
            send_sem=dkv_send.at[n, 4], recv_sem=dkv_recv.at[3 * core + n, 1],
            device_id={"height": sibling}, device_id_type=MESH,
        )

    def oq_copy(n):
        return pltpu.make_async_remote_copy(
            src_ref=oq.at[n, 1 - inner], dst_ref=oq_all.at[3 * core + n],
            send_sem=oq_send.at[n], recv_sem=oq_recv.at[n],
            device_id={"height": sibling}, device_id_type=MESH,
        )

    def backward(n, group):
        halo = isinstance(group, int) and group == 3
        first, size = (TILE, 1152) if halo else (0, 768)
        js = [2, 5, 8] if halo else [3 * group, 3 * group + 1]
        row = pl.ds(group, 1)
        tokens = keys(n, 3) if halo else kv[n, pl.ds(3 * group, 2)].reshape(2 * TILE, 2 * DIM)
        product = jnp.dot(tokens, qt_s[n, 1, :, first:], preferred_element_type=F32)
        e = eh_s[...] if halo else e_s[n, group]
        weights = e.astype(F32) * m_s[n, row, first:]
        slopes = (weights * (product - m_s[n, 4:5, first:])).astype(BF16)
        ds_s[:size, first:] = slopes
        w_s[:size, first:] = weights.astype(BF16)
        turned = jnp.concatenate([kvt_s[n, j, :DIM] for j in js], 1)
        part = jnp.dot(turned, slopes, preferred_element_type=F32)
        if halo:
            dqt_s[n, :, :TILE] = jnp.zeros((DIM, TILE), F32)
            dqt_s[n, :, TILE:] = part
        else:
            dqt_s[n, :, first:] += part
        rhs = qd[n].reshape(2 * TILE, 2 * DIM)[first:]
        key_part = jnp.dot(ds_s[:size, first:], rhs, preferred_element_type=F32)
        value_part = jnp.dot(w_s[:size, first:], rhs, preferred_element_type=F32)
        lanes = lax.broadcasted_iota(jnp.int32, (size, 2 * DIM), 1)
        both = jnp.where(lanes < DIM, key_part, value_part)
        both = both.astype(BF16)
        for i, j in enumerate(js):
            dkv[n, j] = both[i * TILE:(i + 1) * TILE]

    def groups(n):
        for dt in (-1, 1):
            @pl.when(has[dt])
            def _():
                wait_kv(n, 3 * (dt + 1))
                wait_kv(n, 3 * (dt + 1) + 1)

            @pl.when(has[dt] & (n == 1))
            def _():
                pass_over(1, dt).start()
            forward(n, dt + 1)
            if dt < 0:
                @pl.when(n == 1)
                def _():
                    passes_along(2)
            else:
                @pl.when(n == 0)
                def _():
                    kv_along(2, lambda c: c.start())

    def head(n):
        @pl.when(n == 1)
        def _():
            wait_kv(n, 5)
        for dt in (-1, 1):
            @pl.when(has[dt])
            def _():
                wait_kv(n, 3 * (dt + 1) + 2)
        forward(n, 3)
        m_s[n, 3:4, :TILE] = jnp.full((1, TILE), -FAR, F32)
        l_s[n, 3:4, :TILE] = jnp.zeros((1, TILE), F32)
        tops = m_s[n, 0:4]
        shares = jnp.exp(tops - jnp.max(tops, axis=0, keepdims=True))
        shares = shares / jnp.sum(shares * l_s[n, 0:4], axis=0, keepdims=True)
        out = ot_s[n, 0] * shares[0:1] + ot_s[n, 1] * shares[1:2] + ot_s[n, 2] * shares[2:3]
        out = jnp.concatenate([out[:, :TILE], out[:, TILE:] + ot_s[n, 3, :, TILE:] * shares[3:4, TILE:]], 1)
        out = out.astype(BF16).astype(F32)
        ot_s[n, 0] = out
        m_s[n, 0:4] = shares
        m_s[n, 4:5] = jnp.sum(qt_s[n, 1, DIM:].astype(F32) * out, axis=0, keepdims=True)

        @pl.when(n == 1)
        def _():
            add_along(0)

        backward(n, 3)
        for dt in (-1, 1):
            @pl.when(has[dt] & (n < 2))
            def _():
                along_copy(n, dt).start()

            @pl.when(has[dt] & (n == 2))
            def _():
                over_copy(n, dt).start()

    forward_first = lax.rem(t, 8) == 7

    def sides(n, _):
        for k in range(2):
            dt = jnp.where(forward_first, 1 - 2 * k, 2 * k - 1)
            there = (t + dt >= 0) & (t + dt < tiles_t)
            backward(n, dt + 1)

            @pl.when(there)
            def _():
                dkv_copy(n, dt, 0).start()

            @pl.when(there & (n < 2))
            def _():
                dkv_copy(n, dt, 1).start()
        return 0

    def step(i, _):
        @pl.when(i < NEAR)
        def _():
            groups(i)

        @pl.when(i > 0)
        def _():
            head(i - 1)
        lax.fori_loop(jnp.where(i == NEAR, 1, 0), jnp.where(i == NEAR, NEAR, i % 2), sides, 0)
        return 0

    lax.fori_loop(0, NEAR + 1, step, 0)

    def last(n, _):
        @pl.when(n == 0)
        def _():
            add_along(1)

        @pl.when(n == 1)
        def _():
            dkv_copy(2, 0, 2).start()
            add_over(2)
        backward(n, 1)
        dkv_near_copy(n).start()
        terms[3 * core + n, 1] = dkv[n, 3 + inner]
        both = jnp.concatenate([ot_s[n, 0], dqt_s[n] * 0.125], 0).T.astype(BF16)
        oq[n, 0] = both[:TILE]
        oq[n, 1] = both[TILE:]
        oq_copy(n).start()
        oq_all[3 * core + n] = oq[n, inner]
        return 0

    lax.fori_loop(0, NEAR, last, 0)

    def wait_terms(n):
        wait_term(3 * (1 - core) + n, 1)
        for c in range(2):
            for dt in (-1, 1):
                @pl.when(has[dt])
                def _():
                    wait_term(3 * c + n, 1 + dt)

            @pl.when(inner == 1)
            def _():
                wait_term(3 * c + n, 3)

    def wait_term(n, term):
        pltpu.make_async_remote_copy(
            src_ref=dkv.at[0, 0], dst_ref=terms.at[n, term], send_sem=dkv_send.at[0, 0], recv_sem=dkv_recv.at[n, term],
            device_id={"height": sibling}, device_id_type=MESH,
        ).wait_recv()

    def store(pair, even, odd, a, b):
        cols = slice(pair * 2 * DIM, (pair + 1) * 2 * DIM)
        a[:, cols] = jnp.where(low, even, swap_halves(odd)).astype(BF16)
        b[:, cols] = jnp.where(low, swap_halves(even), odd).astype(BF16)

    def summed(n, from_partner):
        total = terms[n, 0].astype(F32)
        for i in range(1, 4 if from_partner else 3):
            total = total + terms[n, i].astype(F32)
        return total

    def store_sums(pair):
        for side in range(2):
            @pl.when(inner == side)
            def _():
                store(pair, summed(2 * pair, side), summed(2 * pair + 1, side), kg_ref, vg_ref)

    wait_terms(0)
    wait_terms(1)
    store_sums(0)
    for n in range(NEAR):
        pltpu.make_async_remote_copy(
            src_ref=oq.at[n, 0], dst_ref=oq_all.at[3 * (1 - core) + n], send_sem=oq_send.at[n], recv_sem=oq_recv.at[n],
            device_id={"height": sibling}, device_id_type=MESH,
        ).wait_recv()
    for pair in range(HEADS // 2):
        store(pair, oq_all[2 * pair].astype(F32), oq_all[2 * pair + 1].astype(F32), att_ref, qg_ref)
    wait_terms(2)
    store_sums(1)
    store_sums(2)

    def drain(n, _):
        qd_copy(n).wait_send()
        kv_beside(n, lambda c: c.wait_send())
        kv_along(n, lambda c: c.wait_send())
        for dt in (-1, 1):
            @pl.when(has[dt])
            def _():
                for u in range(3):
                    dkv_copy(n, dt, u).wait_send()

                pass_over(n, dt).wait_send()
        dkv_copy(n, 0, 2).wait_send()
        dkv_near_copy(n).wait_send()
        oq_copy(n).wait_send()
        return 0

    lax.fori_loop(0, NEAR, drain, 0)


def handed_on(*refs):
    copies = [pltpu.make_async_copy(refs[i], refs[4 + i], refs[8].at[i]) for i in range(4)]
    for copy in copies:
        copy.start()
    for copy in copies:
        copy.wait()


def local(tiles_t, queries, key_tokens, value_tokens, cotangent, window_mask):
    flat = (TILE, HEADS * DIM)
    anywhere = pl.BlockSpec(memory_space=pl.ANY)
    block = (TILE, 2 * DIM)
    dma = pltpu.SemaphoreType.DMA
    outs = pl.pallas_call(
        functools.partial(kernel, tiles_t),
        out_shape=[pltpu.VMEM(flat, BF16)] * 4,
        in_specs=[anywhere] * 5,
        out_specs=[pl.BlockSpec(memory_space=pltpu.VMEM)] * 4,
        scratch_shapes=[
            pltpu.VMEM((4, *flat), BF16),
            pltpu.VMEM((9, 4, tiles_t), jnp.int32),
            pltpu.VMEM((2, 9, 1, 2 * DIM), F32),
            pltpu.VMEM((HEADS, *block), BF16),
            pltpu.VMEM((HEADS, *block), BF16),
            pltpu.VMEM((NEAR, 9, *block), BF16),
            pltpu.VMEM((NEAR, 2, *block), BF16),
            pltpu.VMEM((NEAR, 9, *block), BF16),
            pltpu.VMEM((2, *block), BF16),
            pltpu.VMEM((2, 2, *block), BF16),
            pltpu.VMEM((HEADS, 4, *block), BF16),
            pltpu.VMEM((NEAR, 2, *block), BF16),
            pltpu.VMEM((HEADS, *block), BF16),
            pltpu.VMEM((NEAR, 3, 768, 768), BF16),
            pltpu.VMEM((1152, 384), BF16),
            pltpu.VMEM((1152, 768), BF16),
            pltpu.VMEM((1152, 768), BF16),
            pltpu.VMEM((NEAR, 4, DIM, 768), F32),
            pltpu.VMEM((NEAR, 8, 768), F32),
            pltpu.VMEM((NEAR, 8, 768), F32),
            pltpu.VMEM((NEAR, 2, 2 * DIM, 768), BF16),
            pltpu.VMEM((NEAR, DIM, 768), F32),
            pltpu.VMEM((NEAR, 9, 2 * DIM, TILE), BF16),
            dma((5,)),
            dma((NEAR, 7)),
            dma((NEAR, 9)),
            dma((NEAR, 2)),
            dma((NEAR,)),
            dma((NEAR,)),
            dma((NEAR, 9)),
            dma((HEADS, 4)),
            dma((2,)),
            dma((2, 2)),
            dma((NEAR,)),
            dma((NEAR,)),
        ],
        compiler_params=pltpu.CompilerParams(
            collective_id=0, has_side_effects=True, vmem_limit_bytes=56 * 1024 * 1024
        ),
    )(
        window_mask.transpose(2, 1, 0),
        queries.reshape(flat), key_tokens.reshape(flat), value_tokens.reshape(flat), cotangent.reshape(flat),
    )
    outs = pl.pallas_call(
        handed_on,
        out_shape=[jax.ShapeDtypeStruct(flat, BF16)] * 4,
        in_specs=[pl.BlockSpec(memory_space=pltpu.VMEM)] * 4,
        out_specs=[anywhere] * 4,
        scratch_shapes=[dma((4,))],
    )(*(pltpu.with_memory_space_constraint(out, pltpu.VMEM) for out in outs))
    return tuple(out.reshape(queries.shape) for out in outs)


def solution(mesh):
    spec = P("tm", "height", None, "heads")
    return jax.shard_map(
        functools.partial(local, mesh.shape["tm"]), mesh=mesh, in_specs=(spec,) * 4 + (P(),), out_specs=(spec,) * 4,
        check_vma=False,
    )
```

```python
import functools

import jax
import jax.numpy as jnp
from jax import lax
from jax.experimental import pallas as pl
from jax.experimental.pallas import tpu as pltpu
from jax.sharding import PartitionSpec as P

MESH = pl.DeviceIdType.MESH
F32 = jnp.float32
BF16 = jnp.bfloat16
DIM = 64
TILE = 384
HEADS = 6
NEAR = 3
FAR = 1e30


def swap_halves(x):
    return pltpu.roll(x, DIM, 1)


def kernel(
    tiles_t,
    mask_hbm, q_hbm, k_hbm, v_hbm, g_hbm,
    att_ref, qg_ref, kg_ref, vg_ref,
    arrays, mask_s, flag_s, kv_own, qd_own, kv, qd, dkv, y_back, z_back, terms, oq, oq_all,
    e_s, eh_s, ds_s, w_s, ot_s, m_s, l_s, qt_s, dqt_s, kvt_s,
    load_sem, kv_send, kv_recv, pass_send, qd_send, qd_recv, dkv_send, dkv_recv, y_recv, z_recv, oq_send, oq_recv,
):
    t = lax.axis_index("tm")
    h = lax.axis_index("height")
    hi = h // 2
    core = h % 2
    inner = jnp.where(hi == 0, core, 1 - core)
    sibling = 2 * hi + 1 - core
    outer_h, inner_h, partner_h = 3 * hi, 1 + hi, 2 - hi
    heights = (outer_h, inner_h, partner_h)
    has = {-1: t > 0, 0: t >= 0, 1: t < tiles_t - 1}

    barrier = pltpu.get_barrier_semaphore()
    for dt in (-1, 0, 1):
        @pl.when(has[dt])
        def _():
            for height in (h, sibling) if dt else (sibling, 2 - 2 * hi, 3 - 2 * hi):
                pl.semaphore_signal(barrier, inc=1, device_id={"tm": t + dt, "height": height}, device_id_type=MESH)

    loads = [
        pltpu.make_async_copy(ref, arrays.at[i], load_sem.at[i]) for i, ref in enumerate((k_hbm, v_hbm, q_hbm, g_hbm))
    ] + [pltpu.make_async_copy(mask_hbm, mask_s, load_sem.at[4])]
    for load in loads:
        load.start()

    lane = lax.broadcasted_iota(jnp.int32, (TILE, 2 * DIM), 1)
    low = lane < DIM
    for load in loads[:2]:
        load.wait()

    def pack(own, first, factor, pair, _):
        cols = pl.ds(pl.multiple_of(pair * 2 * DIM, 2 * DIM), 2 * DIM)
        a = arrays[first, :, cols].astype(F32) * factor
        b = arrays[first + 1, :, cols].astype(F32)
        own[2 * pair] = jnp.where(low, a, swap_halves(b)).astype(BF16)
        own[2 * pair + 1] = jnp.where(low, swap_halves(a), b).astype(BF16)
        return 0

    lax.fori_loop(0, HEADS // 2, functools.partial(pack, kv_own, 0, 1.0), 0)
    for dt in (-1, 1):
        @pl.when(jnp.logical_not(has[dt]))
        def _():
            for n in range(NEAR):
                for u in range(3):
                    kv[n, 3 * (dt + 1) + u] = jnp.zeros((TILE, 2 * DIM), BF16)
            for n in range(HEADS):
                terms[n, 1 + dt] = jnp.zeros((TILE, 2 * DIM), BF16)
            for n in range(2):
                z_back[n, (1 + dt) // 2] = jnp.zeros((TILE, 2 * DIM), BF16)
    for n in range(NEAR):
        kv[n, 3 + inner] = kv_own[3 * core + n]
    count = 3 + 2 * ((t > 0).astype(jnp.int32) + (t < tiles_t - 1).astype(jnp.int32))
    pl.semaphore_wait(barrier, count)

    def qd_copy(n):
        return pltpu.make_async_remote_copy(
            src_ref=qd_own.at[3 * (1 - core) + n], dst_ref=qd.at[n, inner],
            send_sem=qd_send.at[n], recv_sem=qd_recv.at[n],
            device_id={"height": sibling}, device_id_type=MESH,
        )

    def kv_copy(n, dt, to, far=0):
        slot = 3 * (1 - dt) + (2 if far else inner)
        index = 5 + to if far else {-1: to, 0: 2, 1: 3 + to}[dt]
        return pltpu.make_async_remote_copy(
            src_ref=kv_own.at[3 * to + n], dst_ref=kv.at[n, slot],
            send_sem=kv_send.at[n, index], recv_sem=kv_recv.at[n, slot],
            device_id={"tm": t + dt, "height": 2 * (1 - hi if far else hi) + to}, device_id_type=MESH,
        )

    def kv_along(n, act):
        for dt in (-1, 1):
            @pl.when(has[dt])
            def _():
                for to in range(2):
                    act(kv_copy(n, dt, to))

    def kv_beside(n, act):
        act(kv_copy(n, 0, 1 - core))

        @pl.when(inner == 1)
        def _():
            for to in range(2):
                act(kv_copy(n, 0, to, 1))

    def pass_over(n, dt):
        slot = 3 * (dt + 1)
        return pltpu.make_async_remote_copy(
            src_ref=kv.at[n, slot + 1], dst_ref=kv.at[n, slot + 2],
            send_sem=pass_send.at[n, (dt + 1) // 2], recv_sem=kv_recv.at[n, slot + 2],
            device_id={"height": 2 * (1 - hi) + core}, device_id_type=MESH,
        )

    def pass_along(n, dt):
        slot = 3 * (1 - dt) + 2
        return pltpu.make_async_remote_copy(
            src_ref=kv.at[n, 5], dst_ref=kv.at[n, slot],
            send_sem=pass_send.at[n, (dt + 1) // 2], recv_sem=kv_recv.at[n, slot],
            device_id={"tm": t + dt}, device_id_type=MESH,
        )

    kv_along(0, lambda c: c.start())
    for n in range(NEAR):
        kv_beside(n, lambda c: c.start())
    kv_along(1, lambda c: c.start())
    for load in loads[2:]:
        load.wait()
    lax.fori_loop(0, HEADS // 2, functools.partial(pack, qd_own, 2, 0.125), 0)
    for n in range(NEAR):
        qd_copy(n).start()
        qd[n, inner] = qd_own[3 * core + n]
    spot = lax.broadcasted_iota(jnp.int32, (9, 4, tiles_t), 2)
    row = lax.broadcasted_iota(jnp.int32, (9, 4, tiles_t), 1)
    for i, query_h in enumerate((outer_h, inner_h)):
        chosen = jnp.where((spot == t) & (row == query_h), mask_s[...], 0).astype(F32)
        chosen = jnp.sum(jnp.sum(chosen, axis=2, keepdims=True), axis=1, keepdims=True)
        flag_s[i] = jnp.broadcast_to(chosen, (9, 1, 2 * DIM))


    def wait_kv(n, slot):
        pltpu.make_async_remote_copy(
            src_ref=kv_own.at[0], dst_ref=kv.at[n, slot], send_sem=kv_send.at[0, 0], recv_sem=kv_recv.at[n, slot],
            device_id={"height": sibling}, device_id_type=MESH,
        ).wait_recv()

    def passes_along(n):
        wait_kv(n, 5)
        for dt in (-1, 1):
            @pl.when(has[dt])
            def _():
                pass_along(n, dt).start()

    def allowed(dt, u):
        def one(i, query_h, key_h):
            if dt == 0 and i == u:
                return jnp.ones((1, TILE), F32)
            flag = flag_s[i, 3 * (dt + 1) + key_h - query_h + 1] * has[dt].astype(F32)
            return jnp.concatenate([flag] * 3, 1)

        inner_flag = one(1, inner_h, heights[u])
        if u == 2:
            return inner_flag
        return jnp.concatenate([one(0, outer_h, heights[u]), inner_flag], 1)

    def slots(group):
        return [3 * group, 3 * group + 1] if group < 3 else [2, 5, 8]

    def keys(n, group):
        if group < 3:
            return kv[n, 3 * group:3 * group + 2].reshape(2 * TILE, 2 * DIM)
        return jnp.concatenate([kv[n, j] for j in slots(3)], 0)

    def forward(n, group):
        js = slots(group)
        first = 0 if group < 3 else TILE
        for j in js:
            kvt_s[n, j] = kv[n, j].T
        scores = jnp.dot(keys(n, group), qt_s[n, 0, :, first:], preferred_element_type=F32)
        flags = [allowed(j // 3 - 1, j % 3) > 0 for j in js]
        tops = [
            jnp.where(flag, jnp.max(scores[i * TILE:(i + 1) * TILE], axis=0, keepdims=True), -FAR)
            for i, flag in enumerate(flags)
        ]
        top = functools.reduce(jnp.maximum, tops)
        total = 0.0
        parts = []
        for i, flag in enumerate(flags):
            e = jnp.exp(scores[i * TILE:(i + 1) * TILE] - jnp.where(flag, top, FAR))
            total = total + jnp.sum(e, axis=0, keepdims=True)
            parts.append(e.astype(BF16))
        e = jnp.concatenate(parts, 0)
        if group < 3:
            e_s[n, group] = e
        else:
            eh_s[...] = e
        values = jnp.concatenate([kvt_s[n, j, DIM:] for j in js], 1)
        ot_s[n, group, :, first:] = jnp.dot(values, e, preferred_element_type=F32)
        m_s[n, group:group + 1, first:] = top
        l_s[n, group:group + 1, first:] = total

    def centre(n, _):
        wait_kv(n, 4 - inner)
        qd_copy(n).wait_recv()
        turned = qd[n].reshape(2 * TILE, 2 * DIM).astype(F32).T
        zero = jnp.zeros((DIM, 2 * TILE), BF16)
        qt_s[n, 0] = jnp.concatenate([turned[:DIM].astype(BF16), zero], 0)
        qt_s[n, 1] = jnp.concatenate([zero, turned[DIM:].astype(BF16)], 0)
        forward(n, 1)
        return 0

    lax.fori_loop(0, NEAR, centre, 0)
    passes_along(0)

    def dkv_copy(n, dt, u):
        term = 3 if u == 2 else 1 - dt
        return pltpu.make_async_remote_copy(
            src_ref=dkv.at[n, 3 * (dt + 1) + u], dst_ref=terms.at[3 * core + n, term],
            send_sem=dkv_send.at[n, 3 * (dt + 1) + u], recv_sem=dkv_recv.at[3 * core + n, term],
            device_id={"tm": t + dt, "height": heights[u]}, device_id_type=MESH,
        )

    def over_copy(n, dt):
        return pltpu.make_async_remote_copy(
            src_ref=dkv.at[n, 3 * (dt + 1) + 2], dst_ref=y_back.at[(dt + 1) // 2],
            send_sem=dkv_send.at[n, 3 * (dt + 1) + 2], recv_sem=y_recv.at[(dt + 1) // 2],
            device_id={"height": 2 * (1 - hi) + core}, device_id_type=MESH,
        )

    def along_copy(n, dt):
        return pltpu.make_async_remote_copy(
            src_ref=dkv.at[n, 3 * (dt + 1) + 2], dst_ref=z_back.at[n, (1 - dt) // 2],
            send_sem=dkv_send.at[n, 3 * (dt + 1) + 2], recv_sem=z_recv.at[n, (1 - dt) // 2],
            device_id={"tm": t + dt}, device_id_type=MESH,
        )

    def add_along(n):
        for i, dt in enumerate((-1, 1)):
            @pl.when(has[dt])
            def _():
                pltpu.make_async_remote_copy(
                    src_ref=dkv.at[0, 0], dst_ref=z_back.at[n, i], send_sem=dkv_send.at[0, 0],
                    recv_sem=z_recv.at[n, i], device_id={"height": sibling}, device_id_type=MESH,
                ).wait_recv()
        dkv[n, 5] = (dkv[n, 5].astype(F32) + z_back[n, 0].astype(F32) + z_back[n, 1].astype(F32)).astype(BF16)
        dkv_copy(n, 0, 2).start()

    def add_over(n):
        for i, dt in enumerate((-1, 1)):
            @pl.when(has[dt])
            def _():
                pltpu.make_async_remote_copy(
                    src_ref=dkv.at[0, 0], dst_ref=y_back.at[i], send_sem=dkv_send.at[0, 0],
                    recv_sem=y_recv.at[i], device_id={"height": sibling}, device_id_type=MESH,
                ).wait_recv()
                slot = 3 * (dt + 1) + 1
                dkv[n, slot] = (dkv[n, slot].astype(F32) + y_back[i].astype(F32)).astype(BF16)
                dkv_copy(n, dt, 1).start()

    def dkv_near_copy(n):
        return pltpu.make_async_remote_copy(
            src_ref=dkv.at[n, 4 - inner], dst_ref=terms.at[3 * core + n, 1],
            send_sem=dkv_send.at[n, 4], recv_sem=dkv_recv.at[3 * core + n, 1],
            device_id={"height": sibling}, device_id_type=MESH,
        )

    def oq_copy(n):
        return pltpu.make_async_remote_copy(
            src_ref=oq.at[n, 1 - inner], dst_ref=oq_all.at[3 * core + n],
            send_sem=oq_send.at[n], recv_sem=oq_recv.at[n],
            device_id={"height": sibling}, device_id_type=MESH,
        )

    def backward(n, group):
        halo = isinstance(group, int) and group == 3
        first, size = (TILE, 1152) if halo else (0, 768)
        js = [2, 5, 8] if halo else [3 * group, 3 * group + 1]
        row = pl.ds(group, 1)
        tokens = keys(n, 3) if halo else kv[n, pl.ds(3 * group, 2)].reshape(2 * TILE, 2 * DIM)
        product = jnp.dot(tokens, qt_s[n, 1, :, first:], preferred_element_type=F32)
        e = eh_s[...] if halo else e_s[n, group]
        weights = e.astype(F32) * m_s[n, row, first:]
        slopes = (weights * (product - m_s[n, 4:5, first:])).astype(BF16)
        ds_s[:size, first:] = slopes
        w_s[:size, first:] = weights.astype(BF16)
        turned = jnp.concatenate([kvt_s[n, j, :DIM] for j in js], 1)
        part = jnp.dot(turned, slopes, preferred_element_type=F32)
        if halo:
            dqt_s[n, :, :TILE] = jnp.zeros((DIM, TILE), F32)
            dqt_s[n, :, TILE:] = part
        else:
            dqt_s[n, :, first:] += part
        rhs = qd[n].reshape(2 * TILE, 2 * DIM)[first:]
        key_part = jnp.dot(ds_s[:size, first:], rhs, preferred_element_type=F32)
        value_part = jnp.dot(w_s[:size, first:], rhs, preferred_element_type=F32)
        lanes = lax.broadcasted_iota(jnp.int32, (size, 2 * DIM), 1)
        both = jnp.where(lanes < DIM, key_part, value_part)
        both = both.astype(BF16)
        for i, j in enumerate(js):
            dkv[n, j] = both[i * TILE:(i + 1) * TILE]

    def groups(n):
        for dt in (-1, 1):
            @pl.when(has[dt])
            def _():
                wait_kv(n, 3 * (dt + 1))
                wait_kv(n, 3 * (dt + 1) + 1)

            @pl.when(has[dt] & (n == 1))
            def _():
                pass_over(1, dt).start()
            forward(n, dt + 1)
            if dt < 0:
                @pl.when(n == 1)
                def _():
                    passes_along(2)
            else:
                @pl.when(n == 0)
                def _():
                    kv_along(2, lambda c: c.start())

    def head(n):
        @pl.when(n == 1)
        def _():
            wait_kv(n, 5)
        for dt in (-1, 1):
            @pl.when(has[dt])
            def _():
                wait_kv(n, 3 * (dt + 1) + 2)
        forward(n, 3)
        m_s[n, 3:4, :TILE] = jnp.full((1, TILE), -FAR, F32)
        l_s[n, 3:4, :TILE] = jnp.zeros((1, TILE), F32)
        tops = m_s[n, 0:4]
        shares = jnp.exp(tops - jnp.max(tops, axis=0, keepdims=True))
        shares = shares / jnp.sum(shares * l_s[n, 0:4], axis=0, keepdims=True)
        out = ot_s[n, 0] * shares[0:1] + ot_s[n, 1] * shares[1:2] + ot_s[n, 2] * shares[2:3]
        out = jnp.concatenate([out[:, :TILE], out[:, TILE:] + ot_s[n, 3, :, TILE:] * shares[3:4, TILE:]], 1)
        out = out.astype(BF16).astype(F32)
        ot_s[n, 0] = out
        m_s[n, 0:4] = shares
        m_s[n, 4:5] = jnp.sum(qt_s[n, 1, DIM:].astype(F32) * out, axis=0, keepdims=True)

        @pl.when(n == 1)
        def _():
            add_along(0)

        backward(n, 3)
        for dt in (-1, 1):
            @pl.when(has[dt] & (n < 2))
            def _():
                along_copy(n, dt).start()

            @pl.when(has[dt] & (n == 2))
            def _():
                over_copy(n, dt).start()

    forward_first = lax.rem(t, 8) == 7

    def sides(n, _):
        for k in range(2):
            dt = jnp.where(forward_first, 1 - 2 * k, 2 * k - 1)
            there = (t + dt >= 0) & (t + dt < tiles_t)
            backward(n, dt + 1)

            @pl.when(there)
            def _():
                dkv_copy(n, dt, 0).start()

            @pl.when(there & (n < 2))
            def _():
                dkv_copy(n, dt, 1).start()
        return 0

    def step(i, _):
        @pl.when(i < NEAR)
        def _():
            groups(i)

        @pl.when(i > 0)
        def _():
            head(i - 1)
        lax.fori_loop(jnp.where(i == NEAR, 1, 0), jnp.where(i == NEAR, NEAR, i % 2), sides, 0)
        return 0

    lax.fori_loop(0, NEAR + 1, step, 0)

    def last(n, _):
        @pl.when(n == 0)
        def _():
            add_along(1)

        @pl.when(n == 1)
        def _():
            dkv_copy(2, 0, 2).start()
            add_over(2)
        backward(n, 1)
        dkv_near_copy(n).start()
        terms[3 * core + n, 1] = dkv[n, 3 + inner]
        both = jnp.concatenate([ot_s[n, 0], dqt_s[n] * 0.125], 0).T.astype(BF16)
        oq[n, 0] = both[:TILE]
        oq[n, 1] = both[TILE:]
        oq_copy(n).start()
        oq_all[3 * core + n] = oq[n, inner]
        return 0

    lax.fori_loop(0, NEAR, last, 0)

    def wait_terms(n):
        wait_term(3 * (1 - core) + n, 1)
        for c in range(2):
            for dt in (-1, 1):
                @pl.when(has[dt])
                def _():
                    wait_term(3 * c + n, 1 + dt)

            @pl.when(inner == 1)
            def _():
                wait_term(3 * c + n, 3)

    def wait_term(n, term):
        pltpu.make_async_remote_copy(
            src_ref=dkv.at[0, 0], dst_ref=terms.at[n, term], send_sem=dkv_send.at[0, 0], recv_sem=dkv_recv.at[n, term],
            device_id={"height": sibling}, device_id_type=MESH,
        ).wait_recv()

    def store(pair, even, odd, a, b):
        cols = slice(pair * 2 * DIM, (pair + 1) * 2 * DIM)
        a[:, cols] = jnp.where(low, even, swap_halves(odd)).astype(BF16)
        b[:, cols] = jnp.where(low, swap_halves(even), odd).astype(BF16)

    def summed(n, from_partner):
        total = terms[n, 0].astype(F32)
        for i in range(1, 4 if from_partner else 3):
            total = total + terms[n, i].astype(F32)
        return total

    def store_sums(pair):
        for side in range(2):
            @pl.when(inner == side)
            def _():
                store(pair, summed(2 * pair, side), summed(2 * pair + 1, side), kg_ref, vg_ref)

    def wait_oq(n):
        pltpu.make_async_remote_copy(
            src_ref=oq.at[n, 0], dst_ref=oq_all.at[3 * (1 - core) + n], send_sem=oq_send.at[n], recv_sem=oq_recv.at[n],
            device_id={"height": sibling}, device_id_type=MESH,
        ).wait_recv()

    def store_oq(pair):
        store(pair, oq_all[2 * pair].astype(F32), oq_all[2 * pair + 1].astype(F32), att_ref, qg_ref)

    wait_oq(0)
    wait_oq(1)
    store_oq(0)
    wait_terms(0)
    wait_terms(1)
    store_sums(0)
    wait_oq(2)
    store_oq(1)
    store_oq(2)
    wait_terms(2)
    store_sums(1)
    store_sums(2)

    def drain(n, _):
        qd_copy(n).wait_send()
        kv_beside(n, lambda c: c.wait_send())
        kv_along(n, lambda c: c.wait_send())
        for dt in (-1, 1):
            @pl.when(has[dt])
            def _():
                for u in range(3):
                    dkv_copy(n, dt, u).wait_send()

                pass_over(n, dt).wait_send()
        dkv_copy(n, 0, 2).wait_send()
        dkv_near_copy(n).wait_send()
        oq_copy(n).wait_send()
        return 0

    lax.fori_loop(0, NEAR, drain, 0)


def handed_on(*refs):
    copies = [pltpu.make_async_copy(refs[i], refs[4 + i], refs[8].at[i]) for i in range(4)]
    for copy in copies:
        copy.start()
    for copy in copies:
        copy.wait()


def local(tiles_t, queries, key_tokens, value_tokens, cotangent, window_mask):
    flat = (TILE, HEADS * DIM)
    anywhere = pl.BlockSpec(memory_space=pl.ANY)
    block = (TILE, 2 * DIM)
    dma = pltpu.SemaphoreType.DMA
    outs = pl.pallas_call(
        functools.partial(kernel, tiles_t),
        out_shape=[pltpu.VMEM(flat, BF16)] * 4,
        in_specs=[anywhere] * 5,
        out_specs=[pl.BlockSpec(memory_space=pltpu.VMEM)] * 4,
        scratch_shapes=[
            pltpu.VMEM((4, *flat), BF16),
            pltpu.VMEM((9, 4, tiles_t), jnp.int32),
            pltpu.VMEM((2, 9, 1, 2 * DIM), F32),
            pltpu.VMEM((HEADS, *block), BF16),
            pltpu.VMEM((HEADS, *block), BF16),
            pltpu.VMEM((NEAR, 9, *block), BF16),
            pltpu.VMEM((NEAR, 2, *block), BF16),
            pltpu.VMEM((NEAR, 9, *block), BF16),
            pltpu.VMEM((2, *block), BF16),
            pltpu.VMEM((2, 2, *block), BF16),
            pltpu.VMEM((HEADS, 4, *block), BF16),
            pltpu.VMEM((NEAR, 2, *block), BF16),
            pltpu.VMEM((HEADS, *block), BF16),
            pltpu.VMEM((NEAR, 3, 768, 768), BF16),
            pltpu.VMEM((1152, 384), BF16),
            pltpu.VMEM((1152, 768), BF16),
            pltpu.VMEM((1152, 768), BF16),
            pltpu.VMEM((NEAR, 4, DIM, 768), F32),
            pltpu.VMEM((NEAR, 8, 768), F32),
            pltpu.VMEM((NEAR, 8, 768), F32),
            pltpu.VMEM((NEAR, 2, 2 * DIM, 768), BF16),
            pltpu.VMEM((NEAR, DIM, 768), F32),
            pltpu.VMEM((NEAR, 9, 2 * DIM, TILE), BF16),
            dma((5,)),
            dma((NEAR, 7)),
            dma((NEAR, 9)),
            dma((NEAR, 2)),
            dma((NEAR,)),
            dma((NEAR,)),
            dma((NEAR, 9)),
            dma((HEADS, 4)),
            dma((2,)),
            dma((2, 2)),
            dma((NEAR,)),
            dma((NEAR,)),
        ],
        compiler_params=pltpu.CompilerParams(
            collective_id=0, has_side_effects=True, vmem_limit_bytes=56 * 1024 * 1024
        ),
    )(
        window_mask.transpose(2, 1, 0),
        queries.reshape(flat), key_tokens.reshape(flat), value_tokens.reshape(flat), cotangent.reshape(flat),
    )
    outs = pl.pallas_call(
        handed_on,
        out_shape=[jax.ShapeDtypeStruct(flat, BF16)] * 4,
        in_specs=[pl.BlockSpec(memory_space=pltpu.VMEM)] * 4,
        out_specs=[anywhere] * 4,
        scratch_shapes=[dma((4,))],
    )(*(pltpu.with_memory_space_constraint(out, pltpu.VMEM) for out in outs))
    return tuple(out.reshape(queries.shape) for out in outs)


def solution(mesh):
    spec = P("tm", "height", None, "heads")
    return jax.shard_map(
        functools.partial(local, mesh.shape["tm"]), mesh=mesh, in_specs=(spec,) * 4 + (P(),), out_specs=(spec,) * 4,
        check_vma=False,
    )
```
